256 devices in a mesh: ha: 16 (over z, y_lo), ta: 8 (over y_hi, x), col: 2 (over core).
Axes of the slice: x: 4, y: 4 (y_hi: 2, y_lo: 2; y = y_hi * 2 + y_lo), z: 8, core: 2. Of those that a mesh axis runs over, the one named last changes fastest.
Arguments:
- tokens: bfloat16 [64, 448, 28, 128], P(('col', 'ta'), 'ha'), parts along dimension 0, may hold values from -6 to 6
- regions_one: int32 [64, 448, 28], P(('col', 'ta'), 'ha'), parts along dimension 0, may hold values from 0 to 2
- regions_three: int32 [64, 112, 7], P(('col', 'ta'), 'ha'), parts along dimension 0, may hold values from 0 to 2
- gain_one: float32 [128], replicated, may hold values from 0.25 to 1.75
- projection_one: bfloat16 [128, 384], replicated, may hold values from -0.5 to 0.5
- outward_one: bfloat16 [128, 128], replicated, may hold values from -0.5 to 0.5
- table_one: float32 [1183, 4], replicated, may hold values from -4 to 303
- merge_gain_one: float32 [512], replicated, may hold values from 0.25 to 1.75
- merge_weight_one: bfloat16 [512, 256], replicated, may hold values from -0.25 to 0.25
- merge_gain_two: float32 [1024], replicated, may hold values from 0.25 to 1.75
- merge_weight_two: bfloat16 [1024, 512], replicated, may hold values from -0.1875 to 0.1875
- gain_three: float32 [512], replicated, may hold values from 0.25 to 1.75
- projection_three: bfloat16 [512, 1536], replicated, may hold values from -0.25 to 0.25
- outward_three: bfloat16 [512, 512], replicated, may hold values from -0.25 to 0.25
- table_three: float32 [1183, 16], replicated, may hold values from -4 to 303
- cotangent: bfloat16 [64, 112, 7, 512], P(('col', 'ta'), 'ha'), parts along dimension 0, may hold values from -6 to 6
Outputs:
- section_three: bfloat16 [64, 112, 7, 512], P(('col', 'ta'), 'ha'), parts along dimension 0
- grad_tokens: bfloat16 [64, 448, 28, 128], P(('col', 'ta'), 'ha'), parts along dimension 0
The draws below stay inside these ranges and needn't reach their ends.
There are 2 independent parts, one for each index of `col`. The reference program is written for one: setup_inputs(seed, part) draws one part's arguments, and reference() takes and returns one part's arrays. A program takes and returns all parts, laid end to end along the dimension named above; an argument that names none is the same for every part. Nothing has to cross between parts.
Inputs may be any that keep to these rules, and one draw needn't show every extreme that they name: `regions_one`: region ids are free for each position. `regions_three`: region ids are free for each position.
All inputs are finite; a program needn't handle non-finite values.
Results may differ from the reference program's by a relative error of at most 0.03.
Values may be sent and summed in bfloat16 or wider, within the bound.
A program may use at most 192 MiB of HBM per device.

```python
import jax
import jax.numpy as jnp
from jax import lax

C1 = 128
C2 = 256
C3 = 512
HEADS1 = 4
HEADS3 = 16
WT = 4
WS = 7
ST = 2
SS = 3
WIDTH = 28
FRAMES = 32
HEIGHT = 448
NREL = 1183


def hot_table(key, head_count):
    normal_key, choose_key = jax.random.split(key)
    baseline = jnp.clip(jax.random.normal(normal_key, (NREL, head_count), jnp.float32), -4.0, 4.0)
    pair_count = (NREL + 1) // 2
    chosen = (jax.random.uniform(choose_key, (pair_count, head_count), jnp.float32) < 0.005).astype(jnp.float32)
    chosen = jnp.repeat(chosen, 2, axis=0)[:NREL]
    parity = (jnp.arange(NREL) % 2).astype(jnp.float32)[:, None]
    raised = 0.25 * baseline + 2.0 * parity
    return jnp.where(chosen > 0.5, raised, baseline)


def draw_table_one(key, part):
    key = jax.random.fold_in(key, 1)
    return hot_table(key, HEADS1)


def draw_table_three(key, part):
    key = jax.random.fold_in(key, 2)
    return hot_table(key, HEADS3)


def set_ends(result, own_key, least, top_value):
    place = [jax.random.randint(jax.random.fold_in(own_key, axis), (), 0, length) for axis, length in enumerate(result.shape)]
    widest = result.shape.index(max(result.shape))
    neighbour = place[:widest] + [(place[widest] + 1) % result.shape[widest]] + place[widest + 1:]
    return result.at[tuple(place)].set(least).at[tuple(neighbour)].set(top_value)


def steps_of(stream_key, shape, cuts, low, high):
    def one(axis_at, blocks):
        steps = jax.random.uniform(jax.random.fold_in(jax.random.fold_in(stream_key, 6), axis_at), (blocks,), jnp.float32, low / len(cuts), high / len(cuts))
        return jnp.repeat(jnp.exp(steps), shape[axis_at] // blocks).reshape((-1,) + (1,) * (len(shape) - axis_at - 1))

    level = one(*cuts[0])
    for cut in cuts[1:]:
        level = level * one(*cut)
    return level


def scatter_about(key, shape, deviation, most, shards=(), kind=jnp.bfloat16):
    level = steps_of(key, shape, shards, -0.22, 0.18) if shards else 1.0
    values = jax.random.normal(key, shape, jnp.float32) * deviation * level
    return jnp.minimum(jnp.maximum(values, -most), most).astype(kind)


def setup_inputs(seed: int = 0, part: int = 0) -> dict:
    arg_keys = jax.random.split(jax.random.key(seed), 17)
    own_keys = jax.random.split(jax.random.fold_in(arg_keys[16], part), 17)
    return {
        "tokens": scatter_about(own_keys[0], (FRAMES, HEIGHT, WIDTH, C1), 1.0, 6.0, ((0, 8), (1, 16))),
        "regions_one": set_ends(jax.random.randint(own_keys[1], (FRAMES, HEIGHT, WIDTH), 0, 3), jax.random.fold_in(own_keys[1], 1), 0, 2).astype(jnp.int32),
        "regions_three": set_ends(jax.random.randint(own_keys[2], (FRAMES, HEIGHT // 4, WIDTH // 4), 0, 3), jax.random.fold_in(own_keys[2], 1), 0, 2).astype(jnp.int32),
        "gain_one": jnp.clip(1.0 + 0.15 * jax.random.normal(arg_keys[3], (C1,), jnp.float32), 0.25, 1.75),
        "projection_one": scatter_about(arg_keys[4], (C1, 3 * C1), C1 ** -0.5, 0.5),
        "outward_one": scatter_about(arg_keys[5], (C1, C1), C1 ** -0.5, 0.5),
        "table_one": draw_table_one(jax.random.fold_in(arg_keys[16], 71), part),
        "merge_gain_one": jnp.clip(1.0 + 0.15 * jax.random.normal(arg_keys[7], (4 * C1,), jnp.float32), 0.25, 1.75),
        "merge_weight_one": scatter_about(arg_keys[8], (4 * C1, C2), (4 * C1) ** -0.5, 0.25),
        "merge_gain_two": jnp.clip(1.0 + 0.15 * jax.random.normal(arg_keys[9], (4 * C2,), jnp.float32), 0.25, 1.75),
        "merge_weight_two": scatter_about(arg_keys[10], (4 * C2, C3), (4 * C2) ** -0.5, 0.1875),
        "gain_three": jnp.clip(1.0 + 0.15 * jax.random.normal(arg_keys[11], (C3,), jnp.float32), 0.25, 1.75),
        "projection_three": scatter_about(arg_keys[12], (C3, 3 * C3), C3 ** -0.5, 0.25),
        "outward_three": scatter_about(arg_keys[13], (C3, C3), C3 ** -0.5, 0.25),
        "table_three": draw_table_three(jax.random.fold_in(arg_keys[16], 71), part),
        "cotangent": scatter_about(own_keys[15], (FRAMES, HEIGHT // 4, WIDTH // 4, C3), 1.0, 6.0, ((0, 8), (1, 16))),
    }


EPSILON = 1e-05

def layer_norm(values, gain_row):
    widened = values.astype(jnp.float32)
    centred = widened - lax.optimization_barrier(jnp.mean(widened, -1, keepdims=True))
    spread = lax.optimization_barrier(jnp.mean(centred * centred, -1, keepdims=True))
    return (centred * lax.rsqrt(spread + EPSILON) * gain_row).astype(jnp.bfloat16)

def relative_bias(bias_table, window_time, window_side):
    token_count = window_time * window_side * window_side
    positions = jnp.arange(token_count, dtype=jnp.int32)
    time_place = positions // (window_side * window_side)
    row_place = positions // window_side % window_side
    column_place = positions % window_side
    extent = 2 * window_side - 1
    table_index = (time_place[:, None] - time_place[None, :] + window_time - 1) * extent * extent
    table_index = table_index + (row_place[:, None] - row_place[None, :] + window_side - 1) * extent
    table_index = table_index + (column_place[:, None] - column_place[None, :] + window_side - 1)
    picked = jnp.take(jnp.transpose(bias_table), table_index.reshape(-1).astype(jnp.int32), axis=1)
    return picked.reshape(bias_table.shape[1], token_count, token_count)

def to_windows(values, window_time, window_side):
    frames, height, width_cells = values.shape[:3]
    trailing = values.shape[3:]
    blocked = values.reshape((frames // window_time, window_time, height // window_side, window_side, width_cells // window_side, window_side) + trailing)
    extra_dims = tuple(range(6, 6 + len(trailing)))
    blocked = jnp.transpose(blocked, (0, 2, 4, 1, 3, 5) + extra_dims)
    return blocked.reshape((-1, window_time * window_side * window_side) + trailing)

def from_windows(windows, frames, height, width_cells, window_time, window_side):
    trailing = windows.shape[2:]
    blocked = windows.reshape((frames // window_time, height // window_side, width_cells // window_side, window_time, window_side, window_side) + trailing)
    extra_dims = tuple(range(6, 6 + len(trailing)))
    blocked = jnp.transpose(blocked, (0, 3, 1, 4, 2, 5) + extra_dims)
    return blocked.reshape((frames, height, width_cells) + trailing)

def window_attention(inputs, region_ids, projection, outward, bias_block, head_count):
    token_count, channels = inputs.shape
    head_size = channels // head_count
    packed = jnp.dot(inputs, projection, preferred_element_type=jnp.float32).astype(jnp.bfloat16)
    queries = packed[:, :channels].reshape(token_count, head_count, head_size).astype(jnp.float32)
    key_rows = packed[:, channels:2 * channels].reshape(token_count, head_count, head_size).astype(jnp.float32)
    value_rows = packed[:, 2 * channels:].reshape(token_count, head_count, head_size).astype(jnp.float32)
    scores = jnp.einsum('qhd,khd->hqk', queries, key_rows) * head_size ** (-0.5) + bias_block
    same_region = region_ids[:, None] == region_ids[None, :]
    scores = jnp.where(same_region[None], scores, -jnp.inf)
    row_peak = lax.stop_gradient(lax.optimization_barrier(jnp.max(scores, -1, keepdims=True)))
    raised = jnp.exp(scores - row_peak)
    probabilities = (raised / lax.optimization_barrier(jnp.sum(raised, -1, keepdims=True))).astype(jnp.bfloat16)
    attended = jnp.einsum('hqk,khd->qhd', probabilities.astype(jnp.float32), value_rows).astype(jnp.bfloat16)
    return jnp.dot(attended.reshape(token_count, channels), outward, preferred_element_type=jnp.float32).astype(jnp.bfloat16)

def attend(rolled, region_ids, projection, outward, bias_table, head_count):
    frames, height, width_cells, channels = rolled.shape
    bias_block = relative_bias(bias_table, WT, WS)
    windows = to_windows(rolled, WT, WS)
    window_ids = to_windows(region_ids, WT, WS)

    def per_window(operands):
        return window_attention(operands[0], operands[1], projection, outward, bias_block, head_count)
    results = lax.map(jax.checkpoint(per_window), (windows, window_ids))
    return from_windows(results, frames, height, width_cells, WT, WS)

def shifted_attention(normed, region_ids, projection, outward, bias_table, head_count):
    rolled = jnp.roll(normed, (-ST, -SS, -SS), (0, 1, 2))
    mixed_heads = attend(rolled, region_ids, projection, outward, bias_table, head_count)
    return jnp.roll(mixed_heads, (ST, SS, SS), (0, 1, 2))

def merge_patches(values, gain_row, weight):
    frames, height, width_cells, channels = values.shape
    grouped = values.reshape(frames, height // 2, 2, width_cells // 2, 2, channels)
    grouped = jnp.transpose(grouped, (0, 1, 3, 4, 2, 5)).reshape(frames, height // 2, width_cells // 2, 4 * channels)
    return jnp.dot(layer_norm(grouped, gain_row), weight, preferred_element_type=jnp.float32).astype(jnp.bfloat16)

def reference(tokens, regions_one, regions_three, gain_one, projection_one, outward_one, table_one, merge_gain_one, merge_weight_one, merge_gain_two, merge_weight_two, gain_three, projection_three, outward_three, table_three, cotangent):

    def forward(inputs):
        normed_one = layer_norm(inputs, gain_one)
        mixed_one = shifted_attention(normed_one, regions_one, projection_one, outward_one, table_one, HEADS1)
        residual_one = (inputs.astype(jnp.float32) + mixed_one.astype(jnp.float32)).astype(jnp.bfloat16)
        merged_one = merge_patches(residual_one, merge_gain_one, merge_weight_one)
        merged_two = merge_patches(merged_one, merge_gain_two, merge_weight_two)
        normed_three = layer_norm(merged_two, gain_three)
        mixed_three = shifted_attention(normed_three, regions_three, projection_three, outward_three, table_three, HEADS3)
        return (merged_two.astype(jnp.float32) + mixed_three.astype(jnp.float32)).astype(jnp.bfloat16)
    section_three, pullback = jax.vjp(forward, tokens)
    grad_tokens = pullback(cotangent)[0]
    return (section_three, grad_tokens)
```

```python
import functools
import math

import jax
import jax.numpy as jnp
from jax import lax
from jax.experimental import pallas as pl
from jax.experimental.pallas import tpu as pltpu
from jax.sharding import PartitionSpec as P

F32 = jnp.float32
BF16 = jnp.bfloat16

C1 = 128
C3 = 512
HEADS1 = 4
HEADS3 = 16
HEAD = 32
EPSILON = 1e-05

GROUPS = 28
ROWS = 224
LANES = 256
WINDOWS = 20
FIRST = 10
OWN = 28 - FIRST
NEXT = 35 - OWN

LOG2E = math.log2(math.e)
LN2 = math.log(2.0)
SCALE = HEAD**-0.5
LEFT_OUT = 1e30

TABLE_LANES = 1408
DEPTH = 768
ALL_HEADS = HEADS1 + HEADS3


def dot(a, b):
    return jnp.dot(a, b, preferred_element_type=F32)


def dot_t(a, b):
    return lax.dot_general(a, b, (((1,), (1,)), ((), ())), preferred_element_type=F32)


def normalised(x):
    centred = x - jnp.mean(x, -1, keepdims=True)
    inverse = lax.rsqrt(jnp.mean(centred * centred, -1, keepdims=True) + EPSILON)
    return centred * inverse, inverse


def norm_pull(grad, hat, inverse, gain):
    scaled = grad * gain
    mean = jnp.mean(scaled, -1, keepdims=True)
    along = jnp.mean(scaled * hat, -1, keepdims=True)
    return inverse * (scaled - mean - hat * along)


def rounded(x):
    return x.astype(BF16).astype(F32)


def head_mask(head):
    lane = lax.broadcasted_iota(jnp.int32, (1, C1), 1)
    return jnp.where((lane >= HEAD * head) & (lane < HEAD * (head + 1)), 1.0, 0.0).astype(BF16)


def padded(x):
    return jnp.concatenate([x, jnp.zeros((LANES - ROWS, x.shape[1]), x.dtype)], 0)


def attend(q, k, values_t, hot, bias_ref, bias_at, probs_ref, at):
    k_wide = jnp.concatenate([k, hot], 1)
    apart = padded((hot - 1.0) * jnp.array(LEFT_OUT, BF16))
    q = padded(q)
    out = []
    for head in range(4):
        q_wide = jnp.concatenate([q * head_mask(head), apart], 1)
        scores = dot_t(k_wide, q_wide)
        for half in range(2):
            lanes = slice(128 * half, 128 * half + 128)
            place = slice(LANES * head + 128 * half, LANES * head + 128 * half + 128)
            part = scores[:, lanes] + bias_ref[bias_at, :, place]
            raised = jnp.exp2(part - jnp.max(part, 0, keepdims=True))
            share = 1.0 / jnp.sum(raised, 0, keepdims=True)
            probs_ref[at, :, place] = (raised * share).astype(BF16)
        probs = probs_ref[at, :, LANES * head : LANES * head + LANES]
        out.append(dot(values_t[HEAD * head : HEAD * head + HEAD], probs))
    return jnp.concatenate(out, 0)


def attend_pull(d_out, d_out_t, out_t, q, keys_t, values, probs_ref, at):
    product = d_out_t * out_t
    q = padded(q)
    d_values = jnp.zeros((ROWS, C1), F32)
    d_keys = jnp.zeros((ROWS, C1), F32)
    d_queries = []
    for head in range(4):
        rows = slice(HEAD * head, HEAD * head + HEAD)
        mask = head_mask(head)
        d_head = d_out * mask
        probs = probs_ref[at, :, LANES * head : LANES * head + LANES]
        d_probs = dot_t(values, d_head)
        delta = jnp.sum(product[rows], 0, keepdims=True)
        d_scores = (probs.astype(F32) * (d_probs - delta)).astype(BF16)
        d_values += dot(probs, d_head)
        d_keys += dot(d_scores, q * mask)
        d_queries.append(dot(keys_t[rows], d_scores))
    d_q = jnp.transpose(jnp.concatenate(d_queries, 0) * SCALE)[:ROWS]
    return jnp.concatenate([d_q.astype(BF16), (d_keys * LN2).astype(BF16), d_values.astype(BF16)], 1)


def bias_kernel(table_ref, one_ref, three_ref, wide_ref):
    for head in range(ALL_HEADS):
        row = jnp.broadcast_to(table_ref[head : head + 1, :] * LOG2E, (8, TABLE_LANES))
        for frame in range(4):
            start = 14 + 169 * (3 - frame)
            moved = pltpu.roll(row, TABLE_LANES - start, 1, stride=1, stride_axis=0)
            first = (frame * ALL_HEADS + head) * 8
            wide_ref[first : first + 8, :] = moved[:, :DEPTH]
    wide = wide_ref[...]
    high = wide.astype(BF16)
    low = (wide - high.astype(F32)).astype(BF16)
    lane = lax.broadcasted_iota(jnp.int32, (DEPTH, LANES), 1)
    depth = lax.broadcasted_iota(jnp.int32, (DEPTH, LANES), 0)
    group = lane >> 3
    column = lane & 7
    frame = (group * 9363) >> 16
    line = group - 7 * frame
    offset = 169 * frame + 13 * line + column
    valid = (column < 7) & (lane < ROWS)
    for key_line in range(7):
        chosen = valid & (depth == offset + 13 * (6 - key_line))
        chosen = jnp.where(chosen, 1.0, 0.0).astype(BF16)
        picked = dot(high, chosen) + dot(low, chosen)
        for key_frame in range(4):
            to = slice(key_frame * 56 + key_line * 8, key_frame * 56 + key_line * 8 + 8)
            for head in range(ALL_HEADS):
                first = (key_frame * ALL_HEADS + head) * 8
                block = picked[first : first + 8]
                if head < HEADS1:
                    one_ref[0, to, head * LANES : (head + 1) * LANES] = block
                else:
                    group_at, place = divmod(head - HEADS1, 4)
                    three_ref[group_at, to, place * LANES : (place + 1) * LANES] = block


def expand_tables(tables):
    return pl.pallas_call(
        bias_kernel,
        out_shape=(
            jax.ShapeDtypeStruct((1, ROWS, 4 * LANES), F32),
            jax.ShapeDtypeStruct((4, ROWS, 4 * LANES), F32),
        ),
        in_specs=[pl.BlockSpec(memory_space=pltpu.VMEM)],
        out_specs=(pl.BlockSpec(memory_space=pltpu.VMEM), pl.BlockSpec(memory_space=pltpu.VMEM)),
        scratch_shapes=[pltpu.VMEM((4 * ALL_HEADS * 8, DEPTH), F32)],
        compiler_params=pltpu.CompilerParams(vmem_limit_bytes=48 * 2**20),
        cost_estimate=pl.CostEstimate(flops=4 * 10**9, bytes_accessed=6 * 10**6, transcendentals=0),
        name="expand_tables",
    )(tables)


def main_kernel(
    tokens,
    tokens_ta,
    tokens_ha,
    tokens_both,
    cot,
    cot_ta,
    cot_ha,
    cot_both,
    hot_one,
    hot_three,
    bias_one,
    bias_three,
    gain_one,
    projection_one,
    kv_one_t,
    outward_one,
    merge_gain_one,
    merge_weight_one,
    merge_gain_two,
    merge_weight_two,
    gain_three,
    projection_three,
    kv_three_t,
    outward_three,
    section_out,
    grad_out,
    grid,
    folded,
    windows,
    mixed,
    probs_one,
    q_one,
    kt_one,
    v_one,
    out_t_one,
    grouped,
    inverse_one,
    merged,
    probs_three,
    q_three,
    k_three,
    v_three,
    kt_three,
    vt_three,
    out_t_three,
    out_three,
    d_out_three,
    d_out_t_three,
    d_packed_three,
    cot_wide,
):
    def place_row(frame, row, values):
        values = values.astype(F32)
        grid[frame, row, 0:28, :] = values
        grid[frame, row, 28:36, :] = values[0:8]

    def own_rows(row, _):
        for frame in range(2):
            place_row(frame, row, tokens[2 + frame, FIRST + row])
            place_row(2 + frame, row, tokens_ta[frame, row])
        return 0

    def next_rows(row, _):
        for frame in range(2):
            place_row(frame, OWN + row, tokens_ha[frame, row])
            place_row(2 + frame, OWN + row, tokens_both[frame, row])
        return 0

    lax.fori_loop(0, OWN, own_rows, 0)
    lax.fori_loop(0, NEXT, next_rows, 0)

    def cut(k, _):
        for m in range(4):
            for frame in range(4):
                for row in range(7):
                    group = (frame * 7 + row) * 8
                    windows[4 * k + m, group : group + 8, :] = grid[frame, 7 * k + row, 3 + 7 * m : 11 + 7 * m, :]
        return 0

    lax.fori_loop(0, 5, cut, 0)

    def forward_one(at, _):
        x = windows[at]
        hat, _unused = normalised(x)
        normed = (hat * gain_one[...]).astype(BF16)
        packed = dot(normed, projection_one[...])
        packed_t = dot_t(kv_one_t[...], normed).astype(BF16)
        q = (packed[:, :C1] * (SCALE * LOG2E)).astype(BF16)
        v_one[at] = packed[:, 2 * C1 :].astype(BF16)
        q_one[at] = q
        kt_one[at] = packed_t[:C1]
        out_t = attend(q, packed[:, C1 : 2 * C1].astype(BF16), packed_t[C1:], hot_one[at], bias_one, 0, probs_one, at)
        out_t_one[at] = out_t.astype(BF16)
        out = jnp.transpose(out_t)[:ROWS].astype(BF16)
        mixed[at] = rounded(x + rounded(dot(out, outward_one[...])))
        return 0

    lax.fori_loop(0, WINDOWS, forward_one, 0)

    def uncut(k, _):
        for frame in range(4):
            for row in range(7):
                group = (frame * 7 + row) * 8
                folded[frame, 7 * k + row, 28:35, :] = mixed[4 * k, group : group + 7, :]
                second = mixed[4 * k + 1, group : group + 7, :]
                folded[frame, 7 * k + row, 7:14, :] = second
                folded[frame, 7 * k + row, 35:42, :] = second
                folded[frame, 7 * k + row, 14:21, :] = mixed[4 * k + 2, group : group + 7, :]
                folded[frame, 7 * k + row, 21:28, :] = mixed[4 * k + 3, group : group + 7, :]
        return 0

    lax.fori_loop(0, 5, uncut, 0)

    def gather_blocks(frame, _):
        for row in range(7):
            group = (frame * 7 + row) * 8
            for a in range(2):
                for b in range(2):
                    for p in range(2):
                        for q in range(2):
                            block = 2 * q + p
                            grouped[2 * b + a, pl.ds(pl.multiple_of(group, 8), 8), 128 * block : 128 * block + 128] = folded[
                                frame, 2 + 4 * row + 2 * a + p, pl.ds(9 + 2 * b + q, 8, stride=4), :
                            ]
        return 0

    lax.fori_loop(0, 4, gather_blocks, 0)

    for place in range(4):
        hat, inverse = normalised(grouped[place])
        grouped[place] = hat
        inverse_one[place] = jnp.broadcast_to(inverse, (ROWS, 128))
        merged[:, 256 * place : 256 * place + 256] = rounded(
            dot((hat * merge_gain_one[...]).astype(BF16), merge_weight_one[...])
        )
    hat_two, inverse_two = normalised(merged[...])
    merged[...] = hat_two
    merged_two = rounded(dot((hat_two * merge_gain_two[...]).astype(BF16), merge_weight_two[...]))
    hat_three, inverse_three = normalised(merged_two)
    normed_three = (hat_three * gain_three[...]).astype(BF16)

    packed = dot(normed_three, projection_three[...])
    packed_t = dot_t(kv_three_t[...], normed_three).astype(BF16)
    for g in range(4):
        q_three[g] = (packed[:, C1 * g : C1 * g + C1] * (SCALE * LOG2E)).astype(BF16)
        k_three[g] = packed[:, C3 + C1 * g : C3 + C1 * g + C1].astype(BF16)
        v_three[g] = packed[:, 2 * C3 + C1 * g : 2 * C3 + C1 * g + C1].astype(BF16)
        kt_three[g] = packed_t[C1 * g : C1 * g + C1]
        vt_three[g] = packed_t[C3 + C1 * g : C3 + C1 * g + C1]

    def forward_three(g, _):
        out_t = attend(q_three[g], k_three[g], vt_three[g], hot_three[...], bias_three, g, probs_three, g)
        out_t_three[g] = out_t.astype(BF16)
        out_three[g] = jnp.transpose(out_t)[:ROWS].astype(BF16)
        return 0

    lax.fori_loop(0, 4, forward_three, 0)
    out = jnp.concatenate([out_three[g] for g in range(4)], 1)
    section = merged_two + rounded(dot(out, outward_three[...]))
    section_out[...] = section.astype(BF16)

    for frame in range(4):
        for row in range(7):
            if row < 4:
                source = cot[2 + frame, 3 + row] if frame < 2 else cot_ta[frame - 2, row]
            else:
                source = cot_ha[frame, row - 4] if frame < 2 else cot_both[frame - 2, row - 4]
            source = source.astype(F32)
            group = (frame * 7 + row) * 8
            cot_wide[group : group + 4, :] = source[3:7]
            cot_wide[group + 4 : group + 7, :] = source[0:3]
            cot_wide[group + 7 : group + 8, :] = jnp.zeros((1, C3), F32)
    d_section = cot_wide[...]
    d_mixed = padded(d_section.astype(BF16))
    d_out = dot_t(d_mixed, outward_three[...]).astype(BF16)
    d_out_t = dot_t(outward_three[...], d_mixed)
    for g in range(4):
        d_out_three[g] = d_out[:, C1 * g : C1 * g + C1]
        d_out_t_three[g] = d_out_t[C1 * g : C1 * g + C1]

    def backward_three(g, _):
        d_packed_three[g] = attend_pull(
            d_out_three[g],
            d_out_t_three[g],
            out_t_three[g].astype(F32),
            q_three[g],
            kt_three[g],
            v_three[g],
            probs_three,
            g,
        )
        return 0

    lax.fori_loop(0, 4, backward_three, 0)
    d_packed = jnp.concatenate(
        [d_packed_three[g, :, C1 * part : C1 * part + C1] for part in range(3) for g in range(4)], 1
    )
    d_normed = rounded(dot_t(d_packed, projection_three[...]))
    d_merged_two = d_section + rounded(norm_pull(d_normed, hat_three, inverse_three, gain_three[...]))
    d_grouped_two = dot_t(d_merged_two.astype(BF16), merge_weight_two[...])
    d_merged_one = norm_pull(d_grouped_two, merged[...], inverse_two, merge_gain_two[...]).astype(BF16)
    for place in range(4):
        d_grouped = dot_t(d_merged_one[:, 256 * place : 256 * place + 256], merge_weight_one[...])
        grouped[place] = norm_pull(d_grouped, grouped[place], inverse_one[place][:, :1], merge_gain_one[...])

    for frame in range(4):
        for row in (0, 1, 30, 31, 32, 33, 34):
            folded[frame, row] = jnp.zeros((48, C1), F32)

    def scatter_blocks(frame, _):
        for row in range(7):
            group = (frame * 7 + row) * 8
            for a in range(2):
                for b in range(2):
                    for p in range(2):
                        for q in range(2):
                            block = 2 * q + p
                            folded[frame, 2 + 4 * row + 2 * a + p, pl.ds(9 + 2 * b + q, 8, stride=4), :] = grouped[
                                2 * b + a, pl.ds(pl.multiple_of(group, 8), 8), 128 * block : 128 * block + 128
                            ]
        return 0

    lax.fori_loop(0, 4, scatter_blocks, 0)

    def cut_back(k, _):
        for frame in range(4):
            for row in range(7):
                group = (frame * 7 + row) * 8
                folded[frame, 7 * k + row, 7:9, :] = folded[frame, 7 * k + row, 35:37, :]
                mixed[4 * k, group : group + 8, :] = folded[frame, 7 * k + row, 28:36, :]
                for m in range(1, 4):
                    mixed[4 * k + m, group : group + 8, :] = folded[frame, 7 * k + row, 7 * m : 7 * m + 8, :]
        return 0

    lax.fori_loop(0, 5, cut_back, 0)

    def backward_one(at, _):
        hat, inverse = normalised(windows[at])
        d_residual = rounded(mixed[at])
        d_mixed = padded(d_residual.astype(BF16))
        d_out = dot_t(d_mixed, outward_one[...]).astype(BF16)
        d_out_t = dot_t(outward_one[...], d_mixed)
        d_packed = attend_pull(
            d_out, d_out_t, out_t_one[at].astype(F32), q_one[at], kt_one[at], v_one[at], probs_one, at
        )
        d_normed = rounded(dot_t(d_packed, projection_one[...]))
        mixed[at] = d_residual + norm_pull(d_normed, hat, inverse, gain_one[...])
        return 0

    lax.fori_loop(0, WINDOWS, backward_one, 0)

    def place_back(k, _):
        for frame in range(4):
            for row in range(7):
                group = (frame * 7 + row) * 8
                for m in range(3):
                    grid[frame, 7 * k + row, 3 + 7 * m : 10 + 7 * m, :] = mixed[4 * k + m, group : group + 7, :]
                grid[frame, 7 * k + row, 24:28, :] = mixed[4 * k + 3, group : group + 4, :]
                grid[frame, 7 * k + row, 0:3, :] = mixed[4 * k + 3, group + 4 : group + 7, :]
                grad_out[frame, 7 * k + row] = grid[frame, 7 * k + row, 0:28, :].astype(BF16)
        return 0

    lax.fori_loop(0, 5, place_back, 0)


def main_call(*operands):
    vmem = pl.BlockSpec(memory_space=pltpu.VMEM)
    return pl.pallas_call(
        main_kernel,
        out_shape=(
            jax.ShapeDtypeStruct((ROWS, C3), BF16),
            jax.ShapeDtypeStruct((4, 35, 28, C1), BF16),
        ),
        in_specs=[vmem] * len(operands),
        out_specs=(vmem, vmem),
        scratch_shapes=[
            pltpu.VMEM((4, 35, 40, C1), F32),
            pltpu.VMEM((4, 35, 48, C1), F32),
            pltpu.VMEM((WINDOWS, ROWS, C1), F32),
            pltpu.VMEM((WINDOWS, ROWS, C1), F32),
            pltpu.VMEM((WINDOWS, ROWS, 4 * LANES), BF16),
            pltpu.VMEM((WINDOWS, ROWS, C1), BF16),
            pltpu.VMEM((WINDOWS, C1, ROWS), BF16),
            pltpu.VMEM((WINDOWS, ROWS, C1), BF16),
            pltpu.VMEM((WINDOWS, C1, LANES), BF16),
            pltpu.VMEM((4, ROWS, 512), F32),
            pltpu.VMEM((4, ROWS, 128), F32),
            pltpu.VMEM((ROWS, 1024), F32),
            pltpu.VMEM((4, ROWS, 4 * LANES), BF16),
            pltpu.VMEM((4, ROWS, C1), BF16),
            pltpu.VMEM((4, ROWS, C1), BF16),
            pltpu.VMEM((4, ROWS, C1), BF16),
            pltpu.VMEM((4, C1, ROWS), BF16),
            pltpu.VMEM((4, C1, ROWS), BF16),
            pltpu.VMEM((4, C1, LANES), BF16),
            pltpu.VMEM((4, ROWS, C1), BF16),
            pltpu.VMEM((4, LANES, C1), BF16),
            pltpu.VMEM((4, C1, LANES), F32),
            pltpu.VMEM((4, ROWS, 3 * C1), BF16),
            pltpu.VMEM((ROWS, C3), F32),
        ],
        compiler_params=pltpu.CompilerParams(vmem_limit_bytes=60 * 2**20),
        cost_estimate=pl.CostEstimate(flops=3 * 10**10, bytes_accessed=2 * 10**7, transcendentals=4 * 10**6),
        name="sections",
    )(*operands)


def send(values, ha_by, ta_by):
    ha_count, ta_count = lax.axis_size("ha"), lax.axis_size("ta")
    pairs = []
    for h in range(ha_count):
        for t in range(ta_count):
            to = ((h + ha_by) % ha_count) * ta_count + (t + ta_by) % ta_count
            pairs.append((h * ta_count + t, to))
    return lax.ppermute(values, ("ha", "ta"), pairs)


def one_hot_regions(ids):
    ids = jnp.pad(ids, ((0, 0), (0, 0), (0, 1)), constant_values=3)
    ids = ids.reshape(-1, ROWS)
    return (ids[:, :, None] == jnp.arange(128, dtype=jnp.int32)).astype(BF16)


def per_device(
    tokens,
    regions_one,
    regions_three,
    gain_one,
    projection_one,
    outward_one,
    table_one,
    merge_gain_one,
    merge_weight_one,
    merge_gain_two,
    merge_weight_two,
    gain_three,
    projection_three,
    outward_three,
    table_three,
    cotangent,
):
    tokens_ta = send(tokens[:2, FIRST:], 0, -1)
    tokens_ha = send(tokens[2:, :NEXT], -1, 0)
    tokens_both = send(tokens[:2, :NEXT], -1, -1)
    cot_ta = send(cotangent[:2, 3:], 0, -1)
    cot_ha = send(cotangent[2:, :3], -1, 0)
    cot_both = send(cotangent[:2, :3], -1, -1)
    regions_next = send(regions_one[:, :14], -1, 0)

    tables = jnp.concatenate([table_one, table_three], 1).T
    tables = jnp.pad(tables, ((0, 0), (8, TABLE_LANES - 8 - tables.shape[1])))
    bias_one, bias_three = expand_tables(tables)

    ids = jnp.concatenate([regions_one[:, 7:], regions_next], 1)
    ids = ids.reshape(4, 5, 7, 4, 7).transpose(1, 3, 0, 2, 4).reshape(WINDOWS, GROUPS, 7)
    hot_one = one_hot_regions(ids)
    hot_three = one_hot_regions(regions_three.reshape(1, GROUPS, 7))[0]

    section, grad = main_call(
        tokens,
        tokens_ta,
        tokens_ha,
        tokens_both,
        cotangent,
        cot_ta,
        cot_ha,
        cot_both,
        hot_one,
        hot_three,
        bias_one,
        bias_three,
        gain_one.reshape(1, -1),
        projection_one,
        projection_one[:, C1:].T,
        outward_one,
        merge_gain_one.reshape(1, -1),
        merge_weight_one,
        merge_gain_two.reshape(1, -1),
        merge_weight_two,
        gain_three.reshape(1, -1),
        projection_three,
        projection_three[:, C3:].T,
        outward_three,
    )

    section = section.reshape(4, 7, 8, C3)
    section = jnp.concatenate([section[:, :, 4:7], section[:, :, :4]], 2)
    from_ta = send(section[2:, :4], 0, 1)
    from_ha = send(section[:2, 4:], 1, 0)
    from_both = send(section[2:, 4:], 1, 1)
    finished = jnp.concatenate(
        [jnp.concatenate([from_both, from_ta], 1), jnp.concatenate([from_ha, section[:2, :4]], 1)], 0
    )

    grad_ta = send(grad[2:, :OWN], 0, 1)
    grad_ha = send(grad[:2, OWN:], 1, 0)
    grad_both = send(grad[2:, OWN:], 1, 1)

    def joined(behind, own):
        shared = behind[:, FIRST:].astype(F32) + own[:, : NEXT - FIRST].astype(F32)
        return jnp.concatenate([behind[:, :FIRST], shared.astype(BF16), own[:, NEXT - FIRST :]], 1)

    grad_total = jnp.concatenate([joined(grad_both, grad_ta), joined(grad_ha, grad[:2, :OWN])], 0)
    return (finished, grad_total)


def solution(mesh):
    wide = P(("col", "ta"), "ha", None, None)
    flat = P(("col", "ta"), "ha", None)
    in_specs = (wide, flat, flat) + (P(),) * 12 + (wide,)
    return jax.shard_map(per_device, mesh=mesh, in_specs=in_specs, out_specs=(wide, wide), check_vma=False)
```

```python
import functools
import math

import jax
import jax.numpy as jnp
from jax import lax
from jax.experimental import pallas as pl
from jax.experimental.pallas import tpu as pltpu
from jax.sharding import PartitionSpec as P

F32 = jnp.float32
BF16 = jnp.bfloat16

C1 = 128
C3 = 512
HEADS1 = 4
HEADS3 = 16
HEAD = 32
EPSILON = 1e-05

GROUPS = 28
ROWS = 224
LANES = 256
WINDOWS = 16
FIRST = 10
OWN = 28 - FIRST
CELLS = 48

LOG2E = math.log2(math.e)
LN2 = math.log(2.0)
SCALE = HEAD**-0.5
LEFT_OUT = 1e30

TABLE_LANES = 1408
DEPTH = 768
ALL_HEADS = HEADS1 + HEADS3


def dot(a, b):
    return jnp.dot(a, b, preferred_element_type=F32)


def dot_t(a, b):
    return lax.dot_general(a, b, (((1,), (1,)), ((), ())), preferred_element_type=F32)


def normalised(x):
    centred = x - jnp.mean(x, -1, keepdims=True)
    inverse = lax.rsqrt(jnp.mean(centred * centred, -1, keepdims=True) + EPSILON)
    return centred * inverse, inverse


def norm_pull(grad, hat, inverse, gain):
    scaled = grad * gain
    mean = jnp.mean(scaled, -1, keepdims=True)
    along = jnp.mean(scaled * hat, -1, keepdims=True)
    return inverse * (scaled - mean - hat * along)


def rounded(x):
    return x.astype(BF16).astype(F32)


def head_mask(head):
    lane = lax.broadcasted_iota(jnp.int32, (1, C1), 1)
    return jnp.where((lane >= HEAD * head) & (lane < HEAD * (head + 1)), 1.0, 0.0).astype(BF16)


def padded(x):
    return jnp.concatenate([x, jnp.zeros((LANES - ROWS, x.shape[1]), x.dtype)], 0)


def attend(q, k, values_t, hot, hot_at, bias_ref, bias_at, probs_ref, at):
    k_wide = jnp.concatenate([k, hot], 1)
    lane = lax.broadcasted_iota(jnp.int32, (1, 128), 1)
    chosen = jnp.where((lane >= hot_at) & (lane < hot_at + 4), LEFT_OUT, 0.0).astype(BF16)
    apart = padded((hot - 1.0) * chosen)
    q = padded(q)
    out = []
    for head in range(4):
        q_wide = jnp.concatenate([q * head_mask(head), apart], 1)
        scores = dot_t(k_wide, q_wide)
        for half in range(2):
            lanes = slice(128 * half, 128 * half + 128)
            place = slice(LANES * head + 128 * half, LANES * head + 128 * half + 128)
            part = scores[:, lanes] + bias_ref[bias_at, :, place]
            raised = jnp.exp2(part - jnp.max(part, 0, keepdims=True))
            share = 1.0 / jnp.sum(raised, 0, keepdims=True)
            probs_ref[at, :, place] = (raised * share).astype(BF16)
        probs = probs_ref[at, :, LANES * head : LANES * head + LANES]
        out.append(dot(values_t[HEAD * head : HEAD * head + HEAD], probs))
    return jnp.concatenate(out, 0)


def attend_pull(d_out, d_out_t, out_t, q, keys_t, values, probs_ref, at):
    product = d_out_t * out_t
    q = padded(q)
    d_values = jnp.zeros((ROWS, C1), F32)
    d_keys = jnp.zeros((ROWS, C1), F32)
    d_queries = []
    for head in range(4):
        rows = slice(HEAD * head, HEAD * head + HEAD)
        mask = head_mask(head)
        d_head = d_out * mask
        probs = probs_ref[at, :, LANES * head : LANES * head + LANES]
        d_probs = dot_t(values, d_head)
        delta = jnp.sum(product[rows], 0, keepdims=True)
        d_scores = (probs.astype(F32) * (d_probs - delta)).astype(BF16)
        d_values += dot(probs, d_head)
        d_keys += dot(d_scores, q * mask)
        d_queries.append(dot(keys_t[rows], d_scores))
    d_q = jnp.transpose(jnp.concatenate(d_queries, 0) * SCALE)[:ROWS]
    return jnp.concatenate([d_q.astype(BF16), (d_keys * LN2).astype(BF16), d_values.astype(BF16)], 1)


def expand_tables(table_ref, one_ref, three_ref, wide_ref):
    for head in range(ALL_HEADS):
        row = jnp.broadcast_to(table_ref[head : head + 1, :] * LOG2E, (8, TABLE_LANES))
        for frame in range(4):
            start = 14 + 169 * (3 - frame)
            moved = pltpu.roll(row, TABLE_LANES - start, 1, stride=1, stride_axis=0)
            first = (frame * ALL_HEADS + head) * 8
            wide_ref[first : first + 8, :] = moved[:, :DEPTH]
    wide = wide_ref[...]
    high = wide.astype(BF16)
    low = (wide - high.astype(F32)).astype(BF16)
    lane = lax.broadcasted_iota(jnp.int32, (DEPTH, LANES), 1)
    depth = lax.broadcasted_iota(jnp.int32, (DEPTH, LANES), 0)
    group = lane >> 3
    column = lane & 7
    frame = (group * 9363) >> 16
    line = group - 7 * frame
    offset = 169 * frame + 13 * line + column
    valid = (column < 7) & (lane < ROWS)
    for key_line in range(7):
        chosen = valid & (depth == offset + 13 * (6 - key_line))
        chosen = jnp.where(chosen, 1.0, 0.0).astype(BF16)
        picked = dot(high, chosen) + dot(low, chosen)
        for key_frame in range(4):
            to = slice(key_frame * 56 + key_line * 8, key_frame * 56 + key_line * 8 + 8)
            for head in range(ALL_HEADS):
                first = (key_frame * ALL_HEADS + head) * 8
                block = picked[first : first + 8]
                if head < HEADS1:
                    one_ref[0, to, head * LANES : (head + 1) * LANES] = block
                else:
                    group_at, place = divmod(head - HEADS1, 4)
                    three_ref[group_at, to, place * LANES : (place + 1) * LANES] = block


def main_kernel(
    ha_count,
    ta_count,
    tokens,
    cotangent,
    hot_own,
    tables,
    gain_one,
    projection_one,
    outward_one,
    merge_gain_one,
    merge_weight_one_hbm,
    merge_gain_two,
    merge_weight_two_hbm,
    gain_three,
    projection_three_hbm,
    outward_three_hbm,
    section_out,
    grad_out,
    held,
    cot_held,
    hot,
    seam_out,
    seam_in,
    back_out,
    back_in,
    section_stage,
    grad_stage,
    merge_weight_one,
    merge_weight_two,
    projection_three,
    outward_three,
    kv_one_t,
    kv_three_t,
    bias_one,
    bias_three,
    grid,
    folded,
    windows,
    mixed,
    probs_one,
    q_one,
    kt_one,
    v_one,
    out_t_one,
    grouped,
    inverse_one,
    merged,
    probs_three,
    q_three,
    k_three,
    v_three,
    kt_three,
    vt_three,
    out_t_three,
    out_three,
    d_out_three,
    d_out_t_three,
    d_packed_three,
    cot_wide,
    wide,
    send_sems,
    receive_sems,
    own_sems,
):
    ha, ta = lax.axis_index("ha"), lax.axis_index("ta")
    ha_next, ha_last = lax.rem(ha + 1, ha_count), lax.rem(ha + ha_count - 1, ha_count)
    ta_next, ta_last = lax.rem(ta + 1, ta_count), lax.rem(ta + ta_count - 1, ta_count)

    barrier = pltpu.get_barrier_semaphore()
    ahead = ({"ta": ta_next}, {"ha": ha_next}, {"ha": ha_next, "ta": ta_next})
    behind = ({"ta": ta_last}, {"ha": ha_last}, {"ha": ha_last, "ta": ta_last})

    sent = []

    def remote(source, target, device):
        at = len(sent)
        sent.append(
            pltpu.make_async_remote_copy(
                src_ref=source,
                dst_ref=target,
                send_sem=send_sems.at[at],
                recv_sem=receive_sems.at[at],
                device_id=device,
                device_id_type=pl.DeviceIdType.MESH,
            )
        )
        return sent[-1]

    moved = []

    def local(source, target):
        moved.append(pltpu.make_async_copy(source, target, own_sems.at[len(moved)]))
        return moved[-1]

    tokens_own = local(tokens.at[2:4, FIRST:28], held.at[0:2, 0:OWN])
    cot_own = local(cotangent.at[2:4, 3:7], cot_held.at[0:2, 0:4])
    hot_copy = local(hot_own, hot.at[0])
    weights = [
        local(projection_three_hbm, projection_three),
        local(merge_weight_one_hbm, merge_weight_one),
        local(merge_weight_two_hbm, merge_weight_two),
        local(outward_three_hbm, outward_three),
    ]
    tokens_ta = remote(tokens.at[0:2, FIRST : FIRST + 7], held.at[2:4, 0:7], behind[0])
    tokens_ta_rest = remote(tokens.at[0:2, FIRST + 7 : 28], held.at[2:4, 7:OWN], behind[0])
    tokens_ha = remote(tokens.at[2:4, 0:FIRST], held.at[0:2, OWN:28], behind[1])
    tokens_both = remote(tokens.at[0:2, 0:FIRST], held.at[2:4, OWN:28], behind[2])
    hot_ha = remote(hot_own, hot.at[1], behind[1])
    cot_ta = remote(cotangent.at[0:2, 3:7], cot_held.at[2:4, 0:4], behind[0])
    cot_ha = remote(cotangent.at[2:4, 0:3], cot_held.at[0:2, 4:7], behind[1])
    cot_both = remote(cotangent.at[0:2, 0:3], cot_held.at[2:4, 4:7], behind[2])
    seam = remote(seam_out, seam_in, behind[1])
    back = remote(back_out, back_in, ahead[1])
    section_copies = [
        remote(section_stage.at[2:4, 0:4], section_out.at[0:2, 3:7], ahead[0]),
        remote(section_stage.at[0:2, 4:7], section_out.at[2:4, 0:3], ahead[1]),
        remote(section_stage.at[2:4, 4:7], section_out.at[0:2, 0:3], ahead[2]),
        local(section_stage.at[0:2, 0:4], section_out.at[2:4, 3:7]),
    ]
    grad_copies = {3: [], 2: [], 1: [], 0: []}
    for k, low, high in ((3, 21, 28), (2, 18, 21)):
        to = slice(low - OWN, high - OWN)
        grad_copies[k].append(remote(grad_stage.at[2:4, low:high], grad_out.at[0:2, to], ahead[2]))
        grad_copies[k].append(remote(grad_stage.at[0:2, low:high], grad_out.at[2:4, to], ahead[1]))
    for k, low, high in ((2, 14, 18), (1, 7, 14), (0, 0, 7)):
        to = slice(low + FIRST, high + FIRST)
        grad_copies[k].append(remote(grad_stage.at[2:4, low:high], grad_out.at[0:2, to], ahead[0]))
        grad_copies[k].append(local(grad_stage.at[0:2, low:high], grad_out.at[2:4, to]))

    tokens_own.start()
    for device in ahead + behind:
        pl.semaphore_signal(barrier, inc=1, device_id=device, device_id_type=pl.DeviceIdType.MESH)
    pl.semaphore_wait(barrier, 6)
    for copy in (tokens_ta, tokens_both, tokens_ha, tokens_ta_rest, hot_ha, cot_ta, cot_both, cot_ha):
        copy.start()
    hot_copy.start()
    for copy in weights:
        copy.start()
    cot_own.start()

    expand_tables(tables, bias_one, bias_three, wide)
    for part in range(2):
        weight = projection_one[:, C1 * (part + 1) : C1 * (part + 2)].astype(F32)
        kv_one_t[C1 * part : C1 * part + C1, :] = jnp.transpose(weight).astype(BF16)
    weights[0].wait()
    for part in range(8):
        weight = projection_three[:, C3 + C1 * part : C3 + C1 * part + C1].astype(F32)
        kv_three_t[C1 * part : C1 * part + C1, :] = jnp.transpose(weight).astype(BF16)
    tokens_own.wait()
    hot_copy.wait()

    def forward_one(k, m):
        at = 4 * k + m
        x = windows[at]
        hat, _unused = normalised(x)
        normed = (hat * gain_one[...]).astype(BF16)
        packed = dot(normed, projection_one[...])
        packed_t = dot_t(kv_one_t[...], normed).astype(BF16)
        q = (packed[:, :C1] * (SCALE * LOG2E)).astype(BF16)
        v_one[at] = packed[:, 2 * C1 :].astype(BF16)
        q_one[at] = q
        kt_one[at] = packed_t[:C1]
        hot_at = 4 * (4 * lax.rem(k + 1, 4) + m)
        out_t = attend(
            q,
            packed[:, C1 : 2 * C1].astype(BF16),
            packed_t[C1:],
            hot[k // 3],
            hot_at,
            bias_one,
            0,
            probs_one,
            at,
        )
        out_t_one[at] = out_t.astype(BF16)
        out = jnp.transpose(out_t)[:ROWS].astype(BF16)
        mixed[at] = rounded(x + rounded(dot(out, outward_one[...])))

    def forward_row(k, _):
        @pl.when(k == 0)
        def _():
            tokens_ta.wait_recv()

        @pl.when(k == 1)
        def _():
            tokens_ta_rest.wait_recv()

        @pl.when(k == 2)
        def _():
            tokens_both.wait_recv()
            tokens_ha.wait_recv()

        @pl.when(k == 3)
        def _():
            hot_ha.wait_recv()

        for frame in range(4):
            for row in range(7):
                values = held[frame, 7 * k + row].astype(F32)
                grid[frame, row, 0:28, :] = values
                grid[frame, row, 28:36, :] = values[0:8]
                group = (frame * 7 + row) * 8
                for m in range(4):
                    windows[4 * k + m, group : group + 8, :] = grid[frame, row, 3 + 7 * m : 11 + 7 * m, :]

        def one(m, _):
            forward_one(k, m)
            return 0

        lax.fori_loop(0, 4, one, 0)

        for frame in range(4):
            for row in range(7):
                group = (frame * 7 + row) * 8
                folded[frame, 7 * k + row, 28:35, :] = mixed[4 * k, group : group + 7, :]
                second = mixed[4 * k + 1, group : group + 7, :]
                folded[frame, 7 * k + row, 7:14, :] = second
                folded[frame, 7 * k + row, 35:42, :] = second
                folded[frame, 7 * k + row, 14:21, :] = mixed[4 * k + 2, group : group + 7, :]
                folded[frame, 7 * k + row, 21:28, :] = mixed[4 * k + 3, group : group + 7, :]

        @pl.when(k == 0)
        def _():
            for frame in range(4):
                for row in range(2):
                    seam_out[frame, row] = folded[frame, row].astype(BF16)
            seam.start()

        return 0

    lax.fori_loop(0, 4, forward_row, 0)
    seam.wait_recv()
    for frame in range(4):
        for row in range(2):
            folded[frame, 28 + row] = seam_in[frame, row].astype(F32)
    for copy in weights[1:]:
        copy.wait()

    def gather_blocks(frame, _):
        for row in range(7):
            group = (frame * 7 + row) * 8
            for a in range(2):
                for b in range(2):
                    for p in range(2):
                        for q in range(2):
                            block = 2 * q + p
                            grouped[2 * b + a, pl.ds(pl.multiple_of(group, 8), 8), 128 * block : 128 * block + 128] = folded[
                                frame, 2 + 4 * row + 2 * a + p, pl.ds(9 + 2 * b + q, 8, stride=4), :
                            ]
        return 0

    lax.fori_loop(0, 4, gather_blocks, 0)

    for place in range(4):
        hat, inverse = normalised(grouped[place])
        grouped[place] = hat
        inverse_one[place] = jnp.broadcast_to(inverse, (ROWS, 128))
        merged[:, 256 * place : 256 * place + 256] = rounded(
            dot((hat * merge_gain_one[...]).astype(BF16), merge_weight_one[...])
        )
    hat_two, inverse_two = normalised(merged[...])
    merged[...] = hat_two
    merged_two = rounded(dot((hat_two * merge_gain_two[...]).astype(BF16), merge_weight_two[...]))
    hat_three, inverse_three = normalised(merged_two)
    normed_three = (hat_three * gain_three[...]).astype(BF16)

    packed = dot(normed_three, projection_three[...])
    packed_t = dot_t(kv_three_t[...], normed_three).astype(BF16)
    for g in range(4):
        q_three[g] = (packed[:, C1 * g : C1 * g + C1] * (SCALE * LOG2E)).astype(BF16)
        k_three[g] = packed[:, C3 + C1 * g : C3 + C1 * g + C1].astype(BF16)
        v_three[g] = packed[:, 2 * C3 + C1 * g : 2 * C3 + C1 * g + C1].astype(BF16)
        kt_three[g] = packed_t[C1 * g : C1 * g + C1]
        vt_three[g] = packed_t[C3 + C1 * g : C3 + C1 * g + C1]

    def forward_three(g, _):
        out_t = attend(q_three[g], k_three[g], vt_three[g], hot[0], 64, bias_three, g, probs_three, g)
        out_t_three[g] = out_t.astype(BF16)
        out_three[g] = jnp.transpose(out_t)[:ROWS].astype(BF16)
        return 0

    lax.fori_loop(0, 4, forward_three, 0)
    out = jnp.concatenate([out_three[g] for g in range(4)], 1)
    cot_wide[...] = merged_two + rounded(dot(out, outward_three[...]))
    for frame in range(4):
        for row in range(7):
            group = (frame * 7 + row) * 8
            values = jnp.concatenate([cot_wide[group + 4 : group + 7, :], cot_wide[group : group + 4, :]], 0)
            section_stage[frame, row] = values.astype(BF16)
    for copy in section_copies:
        copy.start()

    cot_own.wait()
    for copy in (cot_ta, cot_both, cot_ha):
        copy.wait_recv()
    for frame in range(4):
        for row in range(7):
            source = cot_held[frame, row].astype(F32)
            group = (frame * 7 + row) * 8
            cot_wide[group : group + 4, :] = source[3:7]
            cot_wide[group + 4 : group + 7, :] = source[0:3]
            cot_wide[group + 7 : group + 8, :] = jnp.zeros((1, C3), F32)
    d_section = cot_wide[...]
    d_mixed = padded(d_section.astype(BF16))
    d_out = dot_t(d_mixed, outward_three[...]).astype(BF16)
    d_out_t = dot_t(outward_three[...], d_mixed)
    for g in range(4):
        d_out_three[g] = d_out[:, C1 * g : C1 * g + C1]
        d_out_t_three[g] = d_out_t[C1 * g : C1 * g + C1]

    def backward_three(g, _):
        d_packed_three[g] = attend_pull(
            d_out_three[g],
            d_out_t_three[g],
            out_t_three[g].astype(F32),
            q_three[g],
            kt_three[g],
            v_three[g],
            probs_three,
            g,
        )
        return 0

    lax.fori_loop(0, 4, backward_three, 0)
    d_packed = jnp.concatenate(
        [d_packed_three[g, :, C1 * part : C1 * part + C1] for part in range(3) for g in range(4)], 1
    )
    d_normed = rounded(dot_t(d_packed, projection_three[...]))
    d_merged_two = d_section + rounded(norm_pull(d_normed, hat_three, inverse_three, gain_three[...]))
    d_grouped_two = dot_t(d_merged_two.astype(BF16), merge_weight_two[...])
    d_merged_one = norm_pull(d_grouped_two, merged[...], inverse_two, merge_gain_two[...]).astype(BF16)
    for place in range(4):
        d_grouped = dot_t(d_merged_one[:, 256 * place : 256 * place + 256], merge_weight_one[...])
        grouped[place] = norm_pull(d_grouped, grouped[place], inverse_one[place][:, :1], merge_gain_one[...])

    def scatter_blocks(frame, _):
        for row in range(7):
            group = (frame * 7 + row) * 8
            for a in range(2):
                for b in range(2):
                    for p in range(2):
                        for q in range(2):
                            block = 2 * q + p
                            folded[frame, 2 + 4 * row + 2 * a + p, pl.ds(9 + 2 * b + q, 8, stride=4), :] = grouped[
                                2 * b + a, pl.ds(pl.multiple_of(group, 8), 8), 128 * block : 128 * block + 128
                            ]
        return 0

    lax.fori_loop(0, 4, scatter_blocks, 0)
    for frame in range(4):
        for row in range(2):
            back_out[frame, row] = folded[frame, 28 + row].astype(BF16)
    back.start()

    def backward_one(at):
        hat, inverse = normalised(windows[at])
        d_residual = rounded(mixed[at])
        d_mixed = padded(d_residual.astype(BF16))
        d_out = dot_t(d_mixed, outward_one[...]).astype(BF16)
        d_out_t = dot_t(outward_one[...], d_mixed)
        d_packed = attend_pull(
            d_out, d_out_t, out_t_one[at].astype(F32), q_one[at], kt_one[at], v_one[at], probs_one, at
        )
        d_normed = rounded(dot_t(d_packed, projection_one[...]))
        mixed[at] = d_residual + norm_pull(d_normed, hat, inverse, gain_one[...])

    def backward_row(step, _):
        k = 3 - step

        @pl.when(k == 0)
        def _():
            back.wait_recv()
            for frame in range(4):
                for row in range(2):
                    folded[frame, row] = back_in[frame, row].astype(F32)

        for frame in range(4):
            for row in range(7):
                group = (frame * 7 + row) * 8
                folded[frame, 7 * k + row, 7:9, :] = folded[frame, 7 * k + row, 35:37, :]
                mixed[4 * k, group : group + 8, :] = folded[frame, 7 * k + row, 28:36, :]
                for m in range(1, 4):
                    mixed[4 * k + m, group : group + 8, :] = folded[frame, 7 * k + row, 7 * m : 7 * m + 8, :]

        def one(m, _):
            backward_one(4 * k + m)
            return 0

        lax.fori_loop(0, 4, one, 0)

        for frame in range(4):
            for row in range(7):
                group = (frame * 7 + row) * 8
                for m in range(3):
                    grid[frame, row, 3 + 7 * m : 10 + 7 * m, :] = mixed[4 * k + m, group : group + 7, :]
                grid[frame, row, 24:28, :] = mixed[4 * k + 3, group : group + 4, :]
                grid[frame, row, 0:3, :] = mixed[4 * k + 3, group + 4 : group + 7, :]
                grad_stage[frame, 7 * k + row] = grid[frame, row, 0:28, :].astype(BF16)

        for at in range(4):

            @pl.when(k == at)
            def _():
                for copy in grad_copies[at]:
                    copy.start()

        return 0

    lax.fori_loop(0, 4, backward_row, 0)

    early = (tokens_ta, tokens_ta_rest, tokens_ha, tokens_both, hot_ha, cot_ta, cot_ha, cot_both, seam, back)
    for copy in early:
        copy.wait_send()
    for copy in section_copies:
        copy.wait()
    for k in (3, 2, 1, 0):
        for copy in grad_copies[k]:
            copy.wait()


def main_call(mesh_shape, *operands):
    vmem = pl.BlockSpec(memory_space=pltpu.VMEM)
    hbm = pl.BlockSpec(memory_space=pl.ANY)
    in_specs = [hbm, hbm, hbm, vmem, vmem, vmem, vmem, vmem, hbm, vmem, hbm, vmem, hbm, hbm]
    return pl.pallas_call(
        functools.partial(main_kernel, *mesh_shape),
        out_shape=(
            jax.ShapeDtypeStruct((4, 7, 7, C3), BF16),
            jax.ShapeDtypeStruct((4, 28, 28, C1), BF16),
        ),
        in_specs=in_specs,
        out_specs=(hbm, hbm),
        scratch_shapes=[
            pltpu.VMEM((4, 28, 28, C1), BF16),
            pltpu.VMEM((4, 7, 7, C3), BF16),
            pltpu.VMEM((2, ROWS, 128), BF16),
            pltpu.VMEM((4, 2, CELLS, C1), BF16),
            pltpu.VMEM((4, 2, CELLS, C1), BF16),
            pltpu.VMEM((4, 2, CELLS, C1), BF16),
            pltpu.VMEM((4, 2, CELLS, C1), BF16),
            pltpu.VMEM((4, 7, 7, C3), BF16),
            pltpu.VMEM((4, 28, 28, C1), BF16),
            pltpu.VMEM((4 * C1, 2 * C1), BF16),
            pltpu.VMEM((8 * C1, C3), BF16),
            pltpu.VMEM((C3, 3 * C3), BF16),
            pltpu.VMEM((C3, C3), BF16),
            pltpu.VMEM((2 * C1, C1), BF16),
            pltpu.VMEM((2 * C3, C3), BF16),
            pltpu.VMEM((1, ROWS, 4 * LANES), F32),
            pltpu.VMEM((4, ROWS, 4 * LANES), F32),
            pltpu.VMEM((4, 7, 40, C1), F32),
            pltpu.VMEM((4, 30, CELLS, C1), F32),
            pltpu.VMEM((WINDOWS, ROWS, C1), F32),
            pltpu.VMEM((WINDOWS, ROWS, C1), F32),
            pltpu.VMEM((WINDOWS, ROWS, 4 * LANES), BF16),
            pltpu.VMEM((WINDOWS, ROWS, C1), BF16),
            pltpu.VMEM((WINDOWS, C1, ROWS), BF16),
            pltpu.VMEM((WINDOWS, ROWS, C1), BF16),
            pltpu.VMEM((WINDOWS, C1, LANES), BF16),
            pltpu.VMEM((4, ROWS, 512), F32),
            pltpu.VMEM((4, ROWS, 128), F32),
            pltpu.VMEM((ROWS, 1024), F32),
            pltpu.VMEM((4, ROWS, 4 * LANES), BF16),
            pltpu.VMEM((4, ROWS, C1), BF16),
            pltpu.VMEM((4, ROWS, C1), BF16),
            pltpu.VMEM((4, ROWS, C1), BF16),
            pltpu.VMEM((4, C1, ROWS), BF16),
            pltpu.VMEM((4, C1, ROWS), BF16),
            pltpu.VMEM((4, C1, LANES), BF16),
            pltpu.VMEM((4, ROWS, C1), BF16),
            pltpu.VMEM((4, LANES, C1), BF16),
            pltpu.VMEM((4, C1, LANES), F32),
            pltpu.VMEM((4, ROWS, 3 * C1), BF16),
            pltpu.VMEM((ROWS, C3), F32),
            pltpu.VMEM((4 * ALL_HEADS * 8, DEPTH), F32),
            pltpu.SemaphoreType.DMA((20,)),
            pltpu.SemaphoreType.DMA((20,)),
            pltpu.SemaphoreType.DMA((12,)),
        ],
        compiler_params=pltpu.CompilerParams(
            vmem_limit_bytes=62 * 2**20, collective_id=0, has_side_effects=True
        ),
        cost_estimate=pl.CostEstimate(flops=3 * 10**10, bytes_accessed=2 * 10**7, transcendentals=4 * 10**6),
        name="sections",
    )(*operands)


def region_classes(regions_one, regions_three):
    ids = regions_one.reshape(4, 4, 7, 4, 7).transpose(0, 2, 4, 1, 3).reshape(4, 7, 7, WINDOWS)
    ids = jnp.concatenate([ids, regions_three[:, :, :, None]], 3)
    ids = jnp.pad(ids, ((0, 0), (0, 0), (0, 1), (0, 32 - WINDOWS - 1)), constant_values=3).reshape(ROWS, 32)
    return (jnp.repeat(ids, 4, 1) == jnp.arange(128, dtype=jnp.int32) % 4).astype(BF16)


def per_device(
    tokens,
    regions_one,
    regions_three,
    gain_one,
    projection_one,
    outward_one,
    table_one,
    merge_gain_one,
    merge_weight_one,
    merge_gain_two,
    merge_weight_two,
    gain_three,
    projection_three,
    outward_three,
    table_three,
    cotangent,
):
    tables = jnp.concatenate([table_one, table_three], 1).T
    tables = jnp.pad(tables, ((0, 0), (8, TABLE_LANES - 8 - tables.shape[1])))
    return main_call(
        (lax.axis_size("ha"), lax.axis_size("ta")),
        tokens,
        cotangent,
        region_classes(regions_one, regions_three),
        tables,
        gain_one.reshape(1, -1),
        projection_one,
        outward_one,
        merge_gain_one.reshape(1, -1),
        merge_weight_one,
        merge_gain_two.reshape(1, -1),
        merge_weight_two,
        gain_three.reshape(1, -1),
        projection_three,
        outward_three,
    )


def solution(mesh):
    wide = P(("col", "ta"), "ha", None, None)
    flat = P(("col", "ta"), "ha", None)
    in_specs = (wide, flat, flat) + (P(),) * 12 + (wide,)
    return jax.shard_map(per_device, mesh=mesh, in_specs=in_specs, out_specs=(wide, wide), check_vma=False)
```

```python
import functools
import math

import jax
import jax.numpy as jnp
from jax import lax
from jax.experimental import pallas as pl
from jax.experimental.pallas import tpu as pltpu
from jax.sharding import PartitionSpec as P

F32 = jnp.float32
BF16 = jnp.bfloat16

C1 = 128
C3 = 512
HEADS1 = 4
HEADS3 = 16
HEAD = 32
EPSILON = 1e-05

GROUPS = 28
ROWS = 224
LANES = 256
WINDOWS = 16
FIRST = 10
OWN = 28 - FIRST
CELLS = 48

LOG2E = math.log2(math.e)
LN2 = math.log(2.0)
SCALE = HEAD**-0.5
LEFT_OUT = 1e30

TABLE_LANES = 1408
OFFSETS = 1183
DEPTH = 768
ALL_HEADS = HEADS1 + HEADS3


def dot(a, b):
    return jnp.dot(a, b, preferred_element_type=F32)


def dot_t(a, b):
    return lax.dot_general(a, b, (((1,), (1,)), ((), ())), preferred_element_type=F32)


def normalised(x):
    centred = x - jnp.mean(x, -1, keepdims=True)
    inverse = lax.rsqrt(jnp.mean(centred * centred, -1, keepdims=True) + EPSILON)
    return centred * inverse, inverse


def norm_pull(grad, hat, inverse, gain):
    scaled = grad * gain
    mean = jnp.mean(scaled, -1, keepdims=True)
    along = jnp.mean(scaled * hat, -1, keepdims=True)
    return inverse * (scaled - mean - hat * along)


def rounded(x):
    return x.astype(BF16).astype(F32)


def head_mask(head):
    lane = lax.broadcasted_iota(jnp.int32, (1, C1), 1)
    return jnp.where((lane >= HEAD * head) & (lane < HEAD * (head + 1)), 1.0, 0.0).astype(BF16)


def padded(x):
    return jnp.concatenate([x, jnp.zeros((LANES - ROWS, x.shape[1]), x.dtype)], 0)


def attend(q, k, values_t, hot, hot_at, bias_ref, bias_at, probs_ref, at):
    lane = lax.broadcasted_iota(jnp.int32, (1, 128), 1)
    chosen = jnp.where((lane >= hot_at) & (lane < hot_at + 4), LEFT_OUT, 0.0).astype(BF16)
    q_wide = jnp.concatenate([padded(q), padded((hot - 1.0) * chosen)], 1)
    k_wide = jnp.concatenate([jnp.concatenate([k * head_mask(head), hot], 1) for head in range(4)], 0)
    scores = dot_t(k_wide, q_wide)
    out = []
    for head in range(4):
        rows = slice(ROWS * head, ROWS * head + ROWS)
        for half in range(2):
            lanes = slice(128 * half, 128 * half + 128)
            part = scores[rows, lanes] + bias_ref[bias_at, rows, lanes]
            raised = jnp.exp2(part - jnp.max(part, 0, keepdims=True))
            share = 1.0 / jnp.sum(raised, 0, keepdims=True)
            probs_ref[at, rows, lanes] = (raised * share).astype(BF16)
        out.append(dot(values_t[HEAD * head : HEAD * head + HEAD], probs_ref[at, rows, :]))
    return jnp.concatenate(out, 0)


def attend_pull(d_out, d_out_t, out_t, q, keys_t, values, probs_ref, at):
    product = d_out_t * out_t
    values = jnp.concatenate([values * head_mask(head) for head in range(4)], 0)
    d_probs = dot_t(values, d_out)
    d_queries = []
    d_scores = []
    for head in range(4):
        rows = slice(ROWS * head, ROWS * head + ROWS)
        own = slice(HEAD * head, HEAD * head + HEAD)
        delta = jnp.sum(product[own], 0, keepdims=True)
        d_scores.append((probs_ref[at, rows, :].astype(F32) * (d_probs[rows] - delta)).astype(BF16))
        d_queries.append(dot(keys_t[own], d_scores[head]))
    all_values = dot(probs_ref[at], d_out)
    all_keys = dot(jnp.concatenate(d_scores, 0), padded(q))
    d_values = pick_heads(all_values)
    d_keys = pick_heads(all_keys) * LN2
    d_q = jnp.transpose(jnp.concatenate(d_queries, 0) * SCALE)[:ROWS]
    return jnp.concatenate([d_q.astype(BF16), d_keys.astype(BF16), d_values.astype(BF16)], 1)


def pick_heads(stacked):
    lane = lax.broadcasted_iota(jnp.int32, (1, C1), 1)
    result = stacked[3 * ROWS :]
    for head in (2, 1, 0):
        result = jnp.where(lane < HEAD * (head + 1), stacked[ROWS * head : ROWS * head + ROWS], result)
    return result


def expand_tables(table_one, table_three, one_ref, three_ref, table_ref, wide_ref):
    table_ref[...] = jnp.zeros((24, TABLE_LANES), F32)
    table_ref[0:HEADS1, 8 : 8 + OFFSETS] = table_one[...]
    table_ref[8:24, 8 : 8 + OFFSETS] = table_three[...]
    for head in range(ALL_HEADS):
        held_at = head if head < HEADS1 else head + 8 - HEADS1
        row = jnp.broadcast_to(table_ref[held_at : held_at + 1, :] * LOG2E, (8, TABLE_LANES))
        for frame in range(4):
            start = 14 + 169 * (3 - frame)
            moved = pltpu.roll(row, TABLE_LANES - start, 1, stride=1, stride_axis=0)
            first = (frame * ALL_HEADS + head) * 8
            wide_ref[first : first + 8, :] = moved[:, :DEPTH]
    wide = wide_ref[...]
    high = wide.astype(BF16)
    low = (wide - high.astype(F32)).astype(BF16)
    lane = lax.broadcasted_iota(jnp.int32, (DEPTH, LANES), 1)
    depth = lax.broadcasted_iota(jnp.int32, (DEPTH, LANES), 0)
    group = lane >> 3
    column = lane & 7
    frame = (group * 9363) >> 16
    line = group - 7 * frame
    offset = 169 * frame + 13 * line + column
    valid = (column < 7) & (lane < ROWS)
    for key_line in range(7):
        chosen = valid & (depth == offset + 13 * (6 - key_line))
        chosen = jnp.where(chosen, 1.0, 0.0).astype(BF16)
        picked = dot(high, chosen) + dot(low, chosen)
        for key_frame in range(4):
            to = key_frame * 56 + key_line * 8
            for head in range(ALL_HEADS):
                first = (key_frame * ALL_HEADS + head) * 8
                block = picked[first : first + 8]
                if head < HEADS1:
                    one_ref[0, head * ROWS + to : head * ROWS + to + 8, :] = block
                else:
                    group_at, place = divmod(head - HEADS1, 4)
                    three_ref[group_at, place * ROWS + to : place * ROWS + to + 8, :] = block


def region_classes(one_ref, three_ref, hot_ref):
    def spread(ref, first, width, lane_of):
        place = lax.broadcasted_iota(jnp.int32, (8, width), 0)
        column = lax.broadcasted_iota(jnp.int32, (8, width), 1)
        own = jnp.where(column - 7 * ((column * 37) >> 8) == place, 1.0, 0.0)
        ids = [ref[first + row, frame : frame + 1, :].astype(F32) * own for frame in range(4) for row in range(7)]
        column = lax.broadcasted_iota(jnp.int32, (width, 128), 0)
        lane = lax.broadcasted_iota(jnp.int32, (width, 128), 1)
        target = jnp.where((lane >> 2) == lane_of + ((column * 37) >> 8), 1.0, 0.0).astype(BF16)
        return dot(jnp.concatenate(ids, 0).astype(BF16), target)

    ids = spread(three_ref, 0, 7, WINDOWS)
    for k in range(4):
        ids += spread(one_ref, 7 * k, 28, 4 * k)
    lane = lax.broadcasted_iota(jnp.int32, (ROWS, 128), 1) & 3
    place = lax.broadcasted_iota(jnp.int32, (ROWS, 128), 0) & 7
    ids = jnp.where(place == 7, 3.0, ids)
    hot_ref[0] = jnp.where(ids == lane.astype(F32), 1.0, 0.0).astype(BF16)


def main_kernel(
    ha_count,
    ta_count,
    tokens,
    cotangent,
    regions_one,
    regions_three,
    table_one,
    table_three,
    gain_one,
    projection_one,
    outward_one,
    merge_gain_one,
    merge_weight_one_hbm,
    merge_gain_two,
    merge_weight_two_hbm,
    gain_three,
    projection_three_hbm,
    outward_three_hbm,
    section_out,
    grad_out,
    held,
    cot_held,
    hot,
    seam_out,
    seam_in,
    back_out,
    back_in,
    section_stage,
    grad_stage,
    merge_weight_one,
    merge_weight_two,
    projection_three,
    outward_three,
    kv_one_t,
    kv_three_t,
    bias_one,
    bias_three,
    grid,
    folded,
    windows,
    mixed,
    probs_one,
    q_one,
    kt_one,
    v_one,
    out_t_one,
    grouped,
    inverse_one,
    merged,
    probs_three,
    q_three,
    k_three,
    v_three,
    kt_three,
    vt_three,
    out_t_three,
    out_three,
    d_out_three,
    d_out_t_three,
    d_packed_three,
    cot_wide,
    tables,
    wide,
    send_sems,
    receive_sems,
    own_sems,
):
    ha, ta = lax.axis_index("ha"), lax.axis_index("ta")
    ha_next, ha_last = lax.rem(ha + 1, ha_count), lax.rem(ha + ha_count - 1, ha_count)
    ta_next, ta_last = lax.rem(ta + 1, ta_count), lax.rem(ta + ta_count - 1, ta_count)

    barrier = pltpu.get_barrier_semaphore()
    ahead = ({"ta": ta_next}, {"ha": ha_next}, {"ha": ha_next, "ta": ta_next})
    behind = ({"ta": ta_last}, {"ha": ha_last}, {"ha": ha_last, "ta": ta_last})

    sent = []

    def remote(source, target, device):
        at = len(sent)
        sent.append(
            pltpu.make_async_remote_copy(
                src_ref=source,
                dst_ref=target,
                send_sem=send_sems.at[at],
                recv_sem=receive_sems.at[at],
                device_id=device,
                device_id_type=pl.DeviceIdType.MESH,
            )
        )
        return sent[-1]

    moved = []

    def local(source, target):
        moved.append(pltpu.make_async_copy(source, target, own_sems.at[len(moved)]))
        return moved[-1]

    tokens_own = local(tokens.at[2:4, FIRST:28], held.at[0:2, 0:OWN])
    cot_own = local(cotangent.at[2:4, 3:7], cot_held.at[0:2, 0:4])
    weights = [
        local(projection_three_hbm, projection_three),
        local(merge_weight_one_hbm, merge_weight_one),
        local(merge_weight_two_hbm, merge_weight_two),
        local(outward_three_hbm, outward_three),
    ]
    tokens_ta = remote(tokens.at[0:2, FIRST : FIRST + 7], held.at[2:4, 0:7], behind[0])
    tokens_ta_rest = remote(tokens.at[0:2, FIRST + 7 : 28], held.at[2:4, 7:OWN], behind[0])
    tokens_ha = remote(tokens.at[2:4, 0:FIRST], held.at[0:2, OWN:28], behind[1])
    tokens_both = remote(tokens.at[0:2, 0:FIRST], held.at[2:4, OWN:28], behind[2])
    hot_ha = remote(hot.at[0], hot.at[1], behind[1])
    cot_ta = remote(cotangent.at[0:2, 3:7], cot_held.at[2:4, 0:4], behind[0])
    cot_ha = remote(cotangent.at[2:4, 0:3], cot_held.at[0:2, 4:7], behind[1])
    cot_both = remote(cotangent.at[0:2, 0:3], cot_held.at[2:4, 4:7], behind[2])
    seam = remote(seam_out, seam_in, behind[1])
    back = remote(back_out, back_in, ahead[1])
    section_copies = [
        remote(section_stage.at[2:4, 0:4], section_out.at[0:2, 3:7], ahead[0]),
        remote(section_stage.at[0:2, 4:7], section_out.at[2:4, 0:3], ahead[1]),
        remote(section_stage.at[2:4, 4:7], section_out.at[0:2, 0:3], ahead[2]),
        local(section_stage.at[0:2, 0:4], section_out.at[2:4, 3:7]),
    ]
    grad_copies = {3: [], 2: [], 1: [], 0: []}
    for k, low, high in ((3, 21, 28), (2, 18, 21)):
        to = slice(low - OWN, high - OWN)
        grad_copies[k].append(remote(grad_stage.at[2:4, low:high], grad_out.at[0:2, to], ahead[2]))
        grad_copies[k].append(remote(grad_stage.at[0:2, low:high], grad_out.at[2:4, to], ahead[1]))
    for k, low, high in ((2, 14, 18), (1, 7, 14), (0, 0, 7)):
        to = slice(low + FIRST, high + FIRST)
        grad_copies[k].append(remote(grad_stage.at[2:4, low:high], grad_out.at[0:2, to], ahead[0]))
        grad_copies[k].append(local(grad_stage.at[0:2, low:high], grad_out.at[2:4, to]))

    tokens_own.start()
    for device in ahead + behind:
        pl.semaphore_signal(barrier, inc=1, device_id=device, device_id_type=pl.DeviceIdType.MESH)
    pl.semaphore_wait(barrier, 6)
    for copy in (tokens_ta, tokens_both, tokens_ha, tokens_ta_rest, cot_ta, cot_both, cot_ha):
        copy.start()
    for copy in weights:
        copy.start()
    cot_own.start()

    region_classes(regions_one, regions_three, hot)
    hot_ha.start()
    expand_tables(table_one, table_three, bias_one, bias_three, tables, wide)
    for part in range(2):
        weight = projection_one[:, C1 * (part + 1) : C1 * (part + 2)].astype(F32)
        kv_one_t[C1 * part : C1 * part + C1, :] = jnp.transpose(weight).astype(BF16)
    weights[0].wait()
    for part in range(8):
        weight = projection_three[:, C3 + C1 * part : C3 + C1 * part + C1].astype(F32)
        kv_three_t[C1 * part : C1 * part + C1, :] = jnp.transpose(weight).astype(BF16)
    tokens_own.wait()

    def forward_one(k, m):
        at = 4 * k + m
        x = windows[at]
        hat, _unused = normalised(x)
        normed = (hat * gain_one[...]).astype(BF16)
        packed = dot(normed, projection_one[...])
        packed_t = dot_t(kv_one_t[...], normed).astype(BF16)
        q = (packed[:, :C1] * (SCALE * LOG2E)).astype(BF16)
        v_one[at] = packed[:, 2 * C1 :].astype(BF16)
        q_one[at] = q
        kt_one[at] = packed_t[:C1]
        hot_at = 4 * (4 * lax.rem(k + 1, 4) + m)
        out_t = attend(
            q,
            packed[:, C1 : 2 * C1].astype(BF16),
            packed_t[C1:],
            hot[k // 3],
            hot_at,
            bias_one,
            0,
            probs_one,
            at,
        )
        out_t_one[at] = out_t.astype(BF16)
        out = jnp.transpose(out_t)[:ROWS].astype(BF16)
        mixed[at] = rounded(x + rounded(dot(out, outward_one[...])))

    def forward_row(k, _):
        @pl.when(k == 0)
        def _():
            tokens_ta.wait_recv()

        @pl.when(k == 1)
        def _():
            tokens_ta_rest.wait_recv()

        @pl.when(k == 2)
        def _():
            tokens_both.wait_recv()
            tokens_ha.wait_recv()

        @pl.when(k == 3)
        def _():
            hot_ha.wait_recv()

        for frame in range(4):
            for row in range(7):
                values = held[frame, 7 * k + row].astype(F32)
                grid[frame, row, 0:28, :] = values
                grid[frame, row, 28:36, :] = values[0:8]
                group = (frame * 7 + row) * 8
                for m in range(4):
                    windows[4 * k + m, group : group + 8, :] = grid[frame, row, 3 + 7 * m : 11 + 7 * m, :]

        def one(m, _):
            forward_one(k, m)
            return 0

        lax.fori_loop(0, 4, one, 0, unroll=4)

        for frame in range(4):
            for row in range(7):
                group = (frame * 7 + row) * 8
                folded[frame, 7 * k + row, 28:35, :] = mixed[4 * k, group : group + 7, :]
                second = mixed[4 * k + 1, group : group + 7, :]
                folded[frame, 7 * k + row, 7:14, :] = second
                folded[frame, 7 * k + row, 35:42, :] = second
                folded[frame, 7 * k + row, 14:21, :] = mixed[4 * k + 2, group : group + 7, :]
                folded[frame, 7 * k + row, 21:28, :] = mixed[4 * k + 3, group : group + 7, :]

        @pl.when(k == 0)
        def _():
            for frame in range(4):
                for row in range(2):
                    seam_out[frame, row] = folded[frame, row].astype(BF16)
            seam.start()

        return 0

    lax.fori_loop(0, 4, forward_row, 0)
    seam.wait_recv()
    for frame in range(4):
        for row in range(2):
            folded[frame, 28 + row] = seam_in[frame, row].astype(F32)
    for copy in weights[1:]:
        copy.wait()

    def gather_blocks(frame, _):
        for row in range(7):
            group = (frame * 7 + row) * 8
            for a in range(2):
                for b in range(2):
                    for p in range(2):
                        for q in range(2):
                            block = 2 * q + p
                            grouped[2 * b + a, pl.ds(pl.multiple_of(group, 8), 8), 128 * block : 128 * block + 128] = folded[
                                frame, 2 + 4 * row + 2 * a + p, pl.ds(9 + 2 * b + q, 8, stride=4), :
                            ]
        return 0

    lax.fori_loop(0, 4, gather_blocks, 0)

    for place in range(4):
        hat, inverse = normalised(grouped[place])
        grouped[place] = hat
        inverse_one[place] = jnp.broadcast_to(inverse, (ROWS, 128))
        merged[:, 256 * place : 256 * place + 256] = rounded(
            dot((hat * merge_gain_one[...]).astype(BF16), merge_weight_one[...])
        )
    hat_two, inverse_two = normalised(merged[...])
    merged[...] = hat_two
    merged_two = rounded(dot((hat_two * merge_gain_two[...]).astype(BF16), merge_weight_two[...]))
    hat_three, inverse_three = normalised(merged_two)
    normed_three = (hat_three * gain_three[...]).astype(BF16)

    packed = dot(normed_three, projection_three[...])
    packed_t = dot_t(kv_three_t[...], normed_three).astype(BF16)
    for g in range(4):
        q_three[g] = (packed[:, C1 * g : C1 * g + C1] * (SCALE * LOG2E)).astype(BF16)
        k_three[g] = packed[:, C3 + C1 * g : C3 + C1 * g + C1].astype(BF16)
        v_three[g] = packed[:, 2 * C3 + C1 * g : 2 * C3 + C1 * g + C1].astype(BF16)
        kt_three[g] = packed_t[C1 * g : C1 * g + C1]
        vt_three[g] = packed_t[C3 + C1 * g : C3 + C1 * g + C1]

    def forward_three(g, _):
        out_t = attend(q_three[g], k_three[g], vt_three[g], hot[0], 64, bias_three, g, probs_three, g)
        out_t_three[g] = out_t.astype(BF16)
        out_three[g] = jnp.transpose(out_t)[:ROWS].astype(BF16)
        return 0

    lax.fori_loop(0, 4, forward_three, 0, unroll=4)
    out = jnp.concatenate([out_three[g] for g in range(4)], 1)
    cot_wide[...] = merged_two + rounded(dot(out, outward_three[...]))
    for frame in range(4):
        for row in range(7):
            group = (frame * 7 + row) * 8
            values = jnp.concatenate([cot_wide[group + 4 : group + 7, :], cot_wide[group : group + 4, :]], 0)
            section_stage[frame, row] = values.astype(BF16)
    for copy in section_copies:
        copy.start()

    cot_own.wait()
    for copy in (cot_ta, cot_both, cot_ha):
        copy.wait_recv()
    for frame in range(4):
        for row in range(7):
            source = cot_held[frame, row].astype(F32)
            group = (frame * 7 + row) * 8
            cot_wide[group : group + 4, :] = source[3:7]
            cot_wide[group + 4 : group + 7, :] = source[0:3]
            cot_wide[group + 7 : group + 8, :] = jnp.zeros((1, C3), F32)
    d_section = cot_wide[...]
    d_mixed = padded(d_section.astype(BF16))
    d_out = dot_t(d_mixed, outward_three[...]).astype(BF16)
    d_out_t = dot_t(outward_three[...], d_mixed)
    for g in range(4):
        d_out_three[g] = d_out[:, C1 * g : C1 * g + C1]
        d_out_t_three[g] = d_out_t[C1 * g : C1 * g + C1]

    def backward_three(g, _):
        d_packed_three[g] = attend_pull(
            d_out_three[g],
            d_out_t_three[g],
            out_t_three[g].astype(F32),
            q_three[g],
            kt_three[g],
            v_three[g],
            probs_three,
            g,
        )
        return 0

    lax.fori_loop(0, 4, backward_three, 0, unroll=4)
    d_packed = jnp.concatenate(
        [d_packed_three[g, :, C1 * part : C1 * part + C1] for part in range(3) for g in range(4)], 1
    )
    d_normed = rounded(dot_t(d_packed, projection_three[...]))
    d_merged_two = d_section + rounded(norm_pull(d_normed, hat_three, inverse_three, gain_three[...]))
    d_grouped_two = dot_t(d_merged_two.astype(BF16), merge_weight_two[...])
    d_merged_one = norm_pull(d_grouped_two, merged[...], inverse_two, merge_gain_two[...]).astype(BF16)
    for place in range(4):
        d_grouped = dot_t(d_merged_one[:, 256 * place : 256 * place + 256], merge_weight_one[...])
        grouped[place] = norm_pull(d_grouped, grouped[place], inverse_one[place][:, :1], merge_gain_one[...])

    def scatter_blocks(frame, _):
        for row in range(7):
            group = (frame * 7 + row) * 8
            for a in range(2):
                for b in range(2):
                    for p in range(2):
                        for q in range(2):
                            block = 2 * q + p
                            folded[frame, 2 + 4 * row + 2 * a + p, pl.ds(9 + 2 * b + q, 8, stride=4), :] = grouped[
                                2 * b + a, pl.ds(pl.multiple_of(group, 8), 8), 128 * block : 128 * block + 128
                            ]
        return 0

    lax.fori_loop(0, 4, scatter_blocks, 0)
    for frame in range(4):
        for row in range(2):
            back_out[frame, row] = folded[frame, 28 + row].astype(BF16)
    back.start()

    def backward_one(at):
        hat, inverse = normalised(windows[at])
        d_residual = rounded(mixed[at])
        d_mixed = padded(d_residual.astype(BF16))
        d_out = dot_t(d_mixed, outward_one[...]).astype(BF16)
        d_out_t = dot_t(outward_one[...], d_mixed)
        d_packed = attend_pull(
            d_out, d_out_t, out_t_one[at].astype(F32), q_one[at], kt_one[at], v_one[at], probs_one, at
        )
        d_normed = rounded(dot_t(d_packed, projection_one[...]))
        mixed[at] = d_residual + norm_pull(d_normed, hat, inverse, gain_one[...])

    def backward_row(step, _):
        k = 3 - step

        @pl.when(k == 0)
        def _():
            back.wait_recv()
            for frame in range(4):
                for row in range(2):
                    folded[frame, row] = back_in[frame, row].astype(F32)

        for frame in range(4):
            for row in range(7):
                group = (frame * 7 + row) * 8
                folded[frame, 7 * k + row, 7:9, :] = folded[frame, 7 * k + row, 35:37, :]
                mixed[4 * k, group : group + 8, :] = folded[frame, 7 * k + row, 28:36, :]
                for m in range(1, 4):
                    mixed[4 * k + m, group : group + 8, :] = folded[frame, 7 * k + row, 7 * m : 7 * m + 8, :]

        def one(m, _):
            backward_one(4 * k + m)
            return 0

        lax.fori_loop(0, 4, one, 0, unroll=4)

        for frame in range(4):
            for row in range(7):
                group = (frame * 7 + row) * 8
                for m in range(3):
                    grid[frame, row, 3 + 7 * m : 10 + 7 * m, :] = mixed[4 * k + m, group : group + 7, :]
                grid[frame, row, 24:28, :] = mixed[4 * k + 3, group : group + 4, :]
                grid[frame, row, 0:3, :] = mixed[4 * k + 3, group + 4 : group + 7, :]
                grad_stage[frame, 7 * k + row] = grid[frame, row, 0:28, :].astype(BF16)

        for at in range(4):

            @pl.when(k == at)
            def _():
                for copy in grad_copies[at]:
                    copy.start()

        return 0

    lax.fori_loop(0, 4, backward_row, 0)

    early = (tokens_ta, tokens_ta_rest, tokens_ha, tokens_both, hot_ha, cot_ta, cot_ha, cot_both, seam, back)
    for copy in early:
        copy.wait_send()
    for copy in section_copies:
        copy.wait()
    for k in (3, 2, 1, 0):
        for copy in grad_copies[k]:
            copy.wait()


def main_call(mesh_shape, *operands):
    vmem = pl.BlockSpec(memory_space=pltpu.VMEM)
    hbm = pl.BlockSpec(memory_space=pl.ANY)
    in_specs = [hbm, hbm, vmem, vmem, vmem, vmem, vmem, vmem, vmem, vmem, hbm, vmem, hbm, vmem, hbm, hbm]
    return pl.pallas_call(
        functools.partial(main_kernel, *mesh_shape),
        out_shape=(
            jax.ShapeDtypeStruct((4, 7, 7, C3), BF16),
            jax.ShapeDtypeStruct((4, 28, 28, C1), BF16),
        ),
        in_specs=in_specs,
        out_specs=(hbm, hbm),
        scratch_shapes=[
            pltpu.VMEM((4, 28, 28, C1), BF16),
            pltpu.VMEM((4, 7, 7, C3), BF16),
            pltpu.VMEM((2, ROWS, 128), BF16),
            pltpu.VMEM((4, 2, CELLS, C1), BF16),
            pltpu.VMEM((4, 2, CELLS, C1), BF16),
            pltpu.VMEM((4, 2, CELLS, C1), BF16),
            pltpu.VMEM((4, 2, CELLS, C1), BF16),
            pltpu.VMEM((4, 7, 7, C3), BF16),
            pltpu.VMEM((4, 28, 28, C1), BF16),
            pltpu.VMEM((4 * C1, 2 * C1), BF16),
            pltpu.VMEM((8 * C1, C3), BF16),
            pltpu.VMEM((C3, 3 * C3), BF16),
            pltpu.VMEM((C3, C3), BF16),
            pltpu.VMEM((2 * C1, C1), BF16),
            pltpu.VMEM((2 * C3, C3), BF16),
            pltpu.VMEM((1, 4 * ROWS, LANES), F32),
            pltpu.VMEM((4, 4 * ROWS, LANES), F32),
            pltpu.VMEM((4, 7, 40, C1), F32),
            pltpu.VMEM((4, 30, CELLS, C1), F32),
            pltpu.VMEM((WINDOWS, ROWS, C1), F32),
            pltpu.VMEM((WINDOWS, ROWS, C1), F32),
            pltpu.VMEM((WINDOWS, 4 * ROWS, LANES), BF16),
            pltpu.VMEM((WINDOWS, ROWS, C1), BF16),
            pltpu.VMEM((WINDOWS, C1, ROWS), BF16),
            pltpu.VMEM((WINDOWS, ROWS, C1), BF16),
            pltpu.VMEM((WINDOWS, C1, LANES), BF16),
            pltpu.VMEM((4, ROWS, 512), F32),
            pltpu.VMEM((4, ROWS, 128), F32),
            pltpu.VMEM((ROWS, 1024), F32),
            pltpu.VMEM((4, 4 * ROWS, LANES), BF16),
            pltpu.VMEM((4, ROWS, C1), BF16),
            pltpu.VMEM((4, ROWS, C1), BF16),
            pltpu.VMEM((4, ROWS, C1), BF16),
            pltpu.VMEM((4, C1, ROWS), BF16),
            pltpu.VMEM((4, C1, ROWS), BF16),
            pltpu.VMEM((4, C1, LANES), BF16),
            pltpu.VMEM((4, ROWS, C1), BF16),
            pltpu.VMEM((4, LANES, C1), BF16),
            pltpu.VMEM((4, C1, LANES), F32),
            pltpu.VMEM((4, ROWS, 3 * C1), BF16),
            pltpu.VMEM((ROWS, C3), F32),
            pltpu.VMEM((24, TABLE_LANES), F32),
            pltpu.VMEM((4 * ALL_HEADS * 8, DEPTH), F32),
            pltpu.SemaphoreType.DMA((20,)),
            pltpu.SemaphoreType.DMA((20,)),
            pltpu.SemaphoreType.DMA((12,)),
        ],
        compiler_params=pltpu.CompilerParams(
            vmem_limit_bytes=62 * 2**20, collective_id=0, has_side_effects=True
        ),
        cost_estimate=pl.CostEstimate(flops=3 * 10**10, bytes_accessed=2 * 10**7, transcendentals=4 * 10**6),
        name="sections",
    )(*operands)


def per_device(
    tokens,
    regions_one,
    regions_three,
    gain_one,
    projection_one,
    outward_one,
    table_one,
    merge_gain_one,
    merge_weight_one,
    merge_gain_two,
    merge_weight_two,
    gain_three,
    projection_three,
    outward_three,
    table_three,
    cotangent,
):
    return main_call(
        (lax.axis_size("ha"), lax.axis_size("ta")),
        tokens,
        cotangent,
        regions_one.transpose(1, 0, 2),
        regions_three.transpose(1, 0, 2),
        table_one.T,
        table_three.T,
        gain_one.reshape(1, -1),
        projection_one,
        outward_one,
        merge_gain_one.reshape(1, -1),
        merge_weight_one,
        merge_gain_two.reshape(1, -1),
        merge_weight_two,
        gain_three.reshape(1, -1),
        projection_three,
        outward_three,
    )


def solution(mesh):
    wide = P(("col", "ta"), "ha", None, None)
    flat = P(("col", "ta"), "ha", None)
    in_specs = (wide, flat, flat) + (P(),) * 12 + (wide,)
    return jax.shard_map(per_device, mesh=mesh, in_specs=in_specs, out_specs=(wide, wide), check_vma=False)
```

```python
import functools
import math

import jax
import jax.numpy as jnp
from jax import lax
from jax.experimental import pallas as pl
from jax.experimental.pallas import tpu as pltpu
from jax.sharding import PartitionSpec as P

F32 = jnp.float32
BF16 = jnp.bfloat16

C1 = 128
C3 = 512
HEADS1 = 4
HEADS3 = 16
HEAD = 32
EPSILON = 1e-05

GROUPS = 28
ROWS = 224
LANES = 256
WINDOWS = 16
FIRST = 10
OWN = 28 - FIRST
CELLS = 48

LOG2E = math.log2(math.e)
LN2 = math.log(2.0)
SCALE = HEAD**-0.5
LEFT_OUT = 1e30

TABLE_LANES = 1408
OFFSETS = 1183
DEPTH = 768
ALL_HEADS = HEADS1 + HEADS3


def dot(a, b):
    return jnp.dot(a, b, preferred_element_type=F32)


def dot_t(a, b):
    return lax.dot_general(a, b, (((1,), (1,)), ((), ())), preferred_element_type=F32)


def normalised(x):
    centred = x - jnp.mean(x, -1, keepdims=True)
    inverse = lax.rsqrt(jnp.mean(centred * centred, -1, keepdims=True) + EPSILON)
    return centred * inverse, inverse


def norm_pull(grad, hat, inverse, gain):
    scaled = grad * gain
    mean = jnp.mean(scaled, -1, keepdims=True)
    along = jnp.mean(scaled * hat, -1, keepdims=True)
    return inverse * (scaled - mean - hat * along)


def rounded(x):
    return x.astype(BF16).astype(F32)


def head_mask(head):
    lane = lax.broadcasted_iota(jnp.int32, (1, C1), 1)
    return jnp.where((lane >= HEAD * head) & (lane < HEAD * (head + 1)), 1.0, 0.0).astype(BF16)


def padded(x):
    return jnp.concatenate([x, jnp.zeros((LANES - ROWS, x.shape[1]), x.dtype)], 0)


def attend(q, k, values_t, hot, hot_at, bias_ref, bias_at, probs_ref, at):
    lane = lax.broadcasted_iota(jnp.int32, (1, 128), 1)
    chosen = jnp.where((lane >= hot_at) & (lane < hot_at + 4), LEFT_OUT, 0.0).astype(BF16)
    q_wide = jnp.concatenate([padded(q), padded((hot - 1.0) * chosen)], 1)
    k_wide = jnp.concatenate([jnp.concatenate([k * head_mask(head), hot], 1) for head in range(4)], 0)
    scores = dot_t(k_wide, q_wide)
    yield
    out = []
    for head in range(4):
        rows = slice(ROWS * head, ROWS * head + ROWS)
        for half in range(2):
            lanes = slice(128 * half, 128 * half + 128)
            part = scores[rows, lanes] + bias_ref[bias_at, rows, lanes]
            raised = jnp.exp2(part - jnp.max(part, 0, keepdims=True))
            share = 1.0 / jnp.sum(raised, 0, keepdims=True)
            probs_ref[at, rows, lanes] = (raised * share).astype(BF16)
        yield
        out.append(dot(values_t[HEAD * head : HEAD * head + HEAD], probs_ref[at, rows, :]))
    return jnp.concatenate(out, 0)


def attend_pull(d_out, d_out_t, out_t, q, keys_t, values, probs_ref, at):
    product = d_out_t * out_t
    values = jnp.concatenate([values * head_mask(head) for head in range(4)], 0)
    d_probs = dot_t(values, d_out)
    yield
    d_queries = []
    d_scores = []
    for head in range(4):
        rows = slice(ROWS * head, ROWS * head + ROWS)
        own = slice(HEAD * head, HEAD * head + HEAD)
        delta = jnp.sum(product[own], 0, keepdims=True)
        d_scores.append((probs_ref[at, rows, :].astype(F32) * (d_probs[rows] - delta)).astype(BF16))
        yield
        d_queries.append(dot(keys_t[own], d_scores[head]))
    all_values = dot(probs_ref[at], d_out)
    all_keys = dot(jnp.concatenate(d_scores, 0), padded(q))
    yield
    d_values = pick_heads(all_values)
    d_keys = pick_heads(all_keys) * LN2
    d_q = jnp.transpose(jnp.concatenate(d_queries, 0) * SCALE)[:ROWS]
    return jnp.concatenate([d_q.astype(BF16), d_keys.astype(BF16), d_values.astype(BF16)], 1)


def together(parts):
    parts = list(parts)
    while parts:
        parts = [part for part in parts if next(part, parts) is None]


def pick_heads(stacked):
    lane = lax.broadcasted_iota(jnp.int32, (1, C1), 1)
    result = stacked[3 * ROWS :]
    for head in (2, 1, 0):
        result = jnp.where(lane < HEAD * (head + 1), stacked[ROWS * head : ROWS * head + ROWS], result)
    return result


def expand_tables(table_one, table_three, one_ref, three_ref, table_ref, wide_ref):
    table_ref[...] = jnp.zeros((24, TABLE_LANES), F32)
    table_ref[0:HEADS1, 8 : 8 + OFFSETS] = table_one[...]
    table_ref[8:24, 8 : 8 + OFFSETS] = table_three[...]
    for head in range(ALL_HEADS):
        held_at = head if head < HEADS1 else head + 8 - HEADS1
        row = jnp.broadcast_to(table_ref[held_at : held_at + 1, :] * LOG2E, (8, TABLE_LANES))
        for frame in range(4):
            start = 14 + 169 * (3 - frame)
            moved = pltpu.roll(row, TABLE_LANES - start, 1, stride=1, stride_axis=0)
            first = (frame * ALL_HEADS + head) * 8
            wide_ref[first : first + 8, :] = moved[:, :DEPTH]
    wide = wide_ref[...]
    high = wide.astype(BF16)
    low = (wide - high.astype(F32)).astype(BF16)
    lane = lax.broadcasted_iota(jnp.int32, (DEPTH, LANES), 1)
    depth = lax.broadcasted_iota(jnp.int32, (DEPTH, LANES), 0)
    group = lane >> 3
    column = lane & 7
    frame = (group * 9363) >> 16
    line = group - 7 * frame
    offset = 169 * frame + 13 * line + column
    valid = (column < 7) & (lane < ROWS)
    for key_line in range(7):
        chosen = valid & (depth == offset + 13 * (6 - key_line))
        chosen = jnp.where(chosen, 1.0, 0.0).astype(BF16)
        picked = dot(high, chosen) + dot(low, chosen)
        for key_frame in range(4):
            to = key_frame * 56 + key_line * 8
            for head in range(ALL_HEADS):
                first = (key_frame * ALL_HEADS + head) * 8
                block = picked[first : first + 8]
                if head < HEADS1:
                    one_ref[0, head * ROWS + to : head * ROWS + to + 8, :] = block
                else:
                    group_at, place = divmod(head - HEADS1, 4)
                    three_ref[group_at, place * ROWS + to : place * ROWS + to + 8, :] = block


def region_classes(one_ref, three_ref, hot_ref):
    def spread(ref, first, width, lane_of):
        place = lax.broadcasted_iota(jnp.int32, (8, width), 0)
        column = lax.broadcasted_iota(jnp.int32, (8, width), 1)
        own = jnp.where(column - 7 * ((column * 37) >> 8) == place, 1.0, 0.0)
        ids = [ref[first + row, frame : frame + 1, :].astype(F32) * own for frame in range(4) for row in range(7)]
        column = lax.broadcasted_iota(jnp.int32, (width, 128), 0)
        lane = lax.broadcasted_iota(jnp.int32, (width, 128), 1)
        target = jnp.where((lane >> 2) == lane_of + ((column * 37) >> 8), 1.0, 0.0).astype(BF16)
        return dot(jnp.concatenate(ids, 0).astype(BF16), target)

    ids = spread(three_ref, 0, 7, WINDOWS)
    for k in range(4):
        ids += spread(one_ref, 7 * k, 28, 4 * k)
    lane = lax.broadcasted_iota(jnp.int32, (ROWS, 128), 1) & 3
    place = lax.broadcasted_iota(jnp.int32, (ROWS, 128), 0) & 7
    ids = jnp.where(place == 7, 3.0, ids)
    hot_ref[0] = jnp.where(ids == lane.astype(F32), 1.0, 0.0).astype(BF16)


def main_kernel(
    ha_count,
    ta_count,
    tokens,
    cotangent,
    regions_one,
    regions_three,
    table_one,
    table_three,
    gain_one,
    projection_one,
    outward_one,
    merge_gain_one,
    merge_weight_one_hbm,
    merge_gain_two,
    merge_weight_two_hbm,
    gain_three,
    projection_three_hbm,
    outward_three_hbm,
    section_out,
    grad_out,
    held,
    cot_rows,
    cot_stage,
    cot_held,
    hot,
    seam_out,
    seam_in,
    back_out,
    back_in,
    section_stage,
    grad_stage,
    merge_weight_one,
    merge_weight_two,
    projection_three,
    outward_three,
    kv_one_t,
    kv_three_t,
    bias_one,
    bias_three,
    grid,
    folded,
    windows,
    mixed,
    probs_one,
    q_one,
    kt_one,
    v_one,
    out_t_one,
    grouped,
    inverse_one,
    merged,
    probs_three,
    q_three,
    k_three,
    v_three,
    kt_three,
    vt_three,
    out_t_three,
    out_three,
    d_out_three,
    d_out_t_three,
    d_packed_three,
    cot_wide,
    tables,
    wide,
    send_sems,
    receive_sems,
    own_sems,
):
    ha, ta = lax.axis_index("ha"), lax.axis_index("ta")
    ha_next, ha_last = lax.rem(ha + 1, ha_count), lax.rem(ha + ha_count - 1, ha_count)
    ta_next, ta_last = lax.rem(ta + 1, ta_count), lax.rem(ta + ta_count - 1, ta_count)

    barrier = pltpu.get_barrier_semaphore()
    ahead = ({"ta": ta_next}, {"ha": ha_next}, {"ha": ha_next, "ta": ta_next})
    behind = ({"ta": ta_last}, {"ha": ha_last}, {"ha": ha_last, "ta": ta_last})

    sent = []

    def remote(source, target, device):
        at = len(sent)
        sent.append(
            pltpu.make_async_remote_copy(
                src_ref=source,
                dst_ref=target,
                send_sem=send_sems.at[at],
                recv_sem=receive_sems.at[at],
                device_id=device,
                device_id_type=pl.DeviceIdType.MESH,
            )
        )
        return sent[-1]

    moved = []

    def local(source, target):
        moved.append(pltpu.make_async_copy(source, target, own_sems.at[len(moved)]))
        return moved[-1]

    tokens_own = local(tokens.at[2:4, FIRST:28], held.at[0:2, 0:OWN])
    cot_own = local(cot_stage.at[2:4, 3:7], cot_held.at[0:2, 0:4])
    weights = [
        local(projection_three_hbm, projection_three),
        local(merge_weight_one_hbm, merge_weight_one),
        local(merge_weight_two_hbm, merge_weight_two),
        local(outward_three_hbm, outward_three),
    ]
    tokens_ta = remote(tokens.at[0:2, FIRST : FIRST + 7], held.at[2:4, 0:7], behind[0])
    tokens_ta_rest = remote(tokens.at[0:2, FIRST + 7 : 28], held.at[2:4, 7:OWN], behind[0])
    tokens_ha = remote(tokens.at[2:4, 0:FIRST], held.at[0:2, OWN:28], behind[1])
    tokens_both = remote(tokens.at[0:2, 0:FIRST], held.at[2:4, OWN:28], behind[2])
    hot_ha = remote(hot.at[0], hot.at[1], behind[1])
    cot_ta = remote(cot_stage.at[0:2, 3:7], cot_held.at[2:4, 0:4], behind[0])
    cot_ha = remote(cot_stage.at[2:4, 0:3], cot_held.at[0:2, 4:7], behind[1])
    cot_both = remote(cot_stage.at[0:2, 0:3], cot_held.at[2:4, 4:7], behind[2])
    seam = remote(seam_out, seam_in, behind[1])
    back = remote(back_out, back_in, ahead[1])
    section_copies = [
        remote(section_stage.at[2:4, 0:4], section_out.at[0:2, 3:7], ahead[0]),
        remote(section_stage.at[0:2, 4:7], section_out.at[2:4, 0:3], ahead[1]),
        remote(section_stage.at[2:4, 4:7], section_out.at[0:2, 0:3], ahead[2]),
        local(section_stage.at[0:2, 0:4], section_out.at[2:4, 3:7]),
    ]
    grad_copies = {3: [], 2: [], 1: [], 0: []}
    for k, low, high in ((3, 21, 28), (2, 18, 21)):
        to = slice(low - OWN, high - OWN)
        grad_copies[k].append(remote(grad_stage.at[2:4, low:high], grad_out.at[0:2, to], ahead[2]))
        grad_copies[k].append(remote(grad_stage.at[0:2, low:high], grad_out.at[2:4, to], ahead[1]))
    for k, low, high in ((2, 14, 18), (1, 7, 14), (0, 0, 7)):
        to = slice(low + FIRST, high + FIRST)
        grad_copies[k].append(remote(grad_stage.at[2:4, low:high], grad_out.at[0:2, to], ahead[0]))
        grad_copies[k].append(local(grad_stage.at[0:2, low:high], grad_out.at[2:4, to]))

    tokens_own.start()
    for device in ahead + behind:
        pl.semaphore_signal(barrier, inc=1, device_id=device, device_id_type=pl.DeviceIdType.MESH)
    pl.semaphore_wait(barrier, 6)
    for copy in (tokens_ta, tokens_both, tokens_ha, tokens_ta_rest):
        copy.start()
    for copy in weights:
        copy.start()

    region_classes(regions_one, regions_three, hot)
    hot_ha.start()
    for row in range(7):
        source = cotangent[row].astype(F32)
        for column in range(7):
            for frame in range(4):
                cot_rows[frame, row, column : column + 1, :] = source[column, frame : frame + 1, :]
        for frame in range(4):
            cot_stage[frame, row] = cot_rows[frame, row].astype(BF16)
    for copy in (cot_ta, cot_both, cot_ha, cot_own):
        copy.start()
    expand_tables(table_one, table_three, bias_one, bias_three, tables, wide)
    for part in range(2):
        weight = projection_one[:, C1 * (part + 1) : C1 * (part + 2)].astype(F32)
        kv_one_t[C1 * part : C1 * part + C1, :] = jnp.transpose(weight).astype(BF16)
    weights[0].wait()
    for part in range(8):
        weight = projection_three[:, C3 + C1 * part : C3 + C1 * part + C1].astype(F32)
        kv_three_t[C1 * part : C1 * part + C1, :] = jnp.transpose(weight).astype(BF16)
    tokens_own.wait()

    def forward_one(k, m):
        at = 4 * k + m
        x = windows[at]
        hat, _unused = normalised(x)
        normed = (hat * gain_one[...]).astype(BF16)
        yield
        packed = dot(normed, projection_one[...])
        packed_t = dot_t(kv_one_t[...], normed).astype(BF16)
        yield
        q = (packed[:, :C1] * (SCALE * LOG2E)).astype(BF16)
        v_one[at] = packed[:, 2 * C1 :].astype(BF16)
        q_one[at] = q
        kt_one[at] = packed_t[:C1]
        hot_at = 4 * (4 * lax.rem(k + 1, 4) + m)
        out_t = yield from attend(
            q,
            packed[:, C1 : 2 * C1].astype(BF16),
            packed_t[C1:],
            hot[k // 3],
            hot_at,
            bias_one,
            0,
            probs_one,
            at,
        )
        yield
        out_t_one[at] = out_t.astype(BF16)
        out = jnp.transpose(out_t)[:ROWS].astype(BF16)
        mixed[at] = rounded(x + rounded(dot(out, outward_one[...])))

    def forward_row(k, _):
        @pl.when(k == 0)
        def _():
            tokens_ta.wait_recv()

        @pl.when(k == 1)
        def _():
            tokens_ta_rest.wait_recv()

        @pl.when(k == 2)
        def _():
            tokens_both.wait_recv()
            tokens_ha.wait_recv()

        @pl.when(k == 3)
        def _():
            hot_ha.wait_recv()

        for frame in range(4):
            for row in range(7):
                values = held[frame, 7 * k + row].astype(F32)
                grid[frame, row, 0:28, :] = values
                grid[frame, row, 28:36, :] = values[0:8]
                group = (frame * 7 + row) * 8
                for m in range(4):
                    windows[4 * k + m, group : group + 8, :] = grid[frame, row, 3 + 7 * m : 11 + 7 * m, :]

        together(forward_one(k, m) for m in range(4))

        for frame in range(4):
            for row in range(7):
                group = (frame * 7 + row) * 8
                folded[frame, 7 * k + row, 28:35, :] = mixed[4 * k, group : group + 7, :]
                second = mixed[4 * k + 1, group : group + 7, :]
                folded[frame, 7 * k + row, 7:14, :] = second
                folded[frame, 7 * k + row, 35:42, :] = second
                folded[frame, 7 * k + row, 14:21, :] = mixed[4 * k + 2, group : group + 7, :]
                folded[frame, 7 * k + row, 21:28, :] = mixed[4 * k + 3, group : group + 7, :]

        @pl.when(k == 0)
        def _():
            for frame in range(4):
                for row in range(2):
                    seam_out[frame, row] = folded[frame, row].astype(BF16)
            seam.start()

        return 0

    lax.fori_loop(0, 4, forward_row, 0)
    seam.wait_recv()
    for frame in range(4):
        for row in range(2):
            folded[frame, 28 + row] = seam_in[frame, row].astype(F32)
    for copy in weights[1:]:
        copy.wait()

    def gather_blocks(frame, _):
        for row in range(7):
            group = (frame * 7 + row) * 8
            for a in range(2):
                for b in range(2):
                    for p in range(2):
                        for q in range(2):
                            block = 2 * q + p
                            grouped[2 * b + a, pl.ds(pl.multiple_of(group, 8), 8), 128 * block : 128 * block + 128] = folded[
                                frame, 2 + 4 * row + 2 * a + p, pl.ds(9 + 2 * b + q, 8, stride=4), :
                            ]
        return 0

    lax.fori_loop(0, 4, gather_blocks, 0)

    for place in range(4):
        hat, inverse = normalised(grouped[place])
        grouped[place] = hat
        inverse_one[place] = jnp.broadcast_to(inverse, (ROWS, 128))
        merged[:, 256 * place : 256 * place + 256] = rounded(
            dot((hat * merge_gain_one[...]).astype(BF16), merge_weight_one[...])
        )
    hat_two, inverse_two = normalised(merged[...])
    merged[...] = hat_two
    merged_two = rounded(dot((hat_two * merge_gain_two[...]).astype(BF16), merge_weight_two[...]))
    hat_three, inverse_three = normalised(merged_two)
    normed_three = (hat_three * gain_three[...]).astype(BF16)

    packed = dot(normed_three, projection_three[...])
    packed_t = dot_t(kv_three_t[...], normed_three).astype(BF16)
    for g in range(4):
        q_three[g] = (packed[:, C1 * g : C1 * g + C1] * (SCALE * LOG2E)).astype(BF16)
        k_three[g] = packed[:, C3 + C1 * g : C3 + C1 * g + C1].astype(BF16)
        v_three[g] = packed[:, 2 * C3 + C1 * g : 2 * C3 + C1 * g + C1].astype(BF16)
        kt_three[g] = packed_t[C1 * g : C1 * g + C1]
        vt_three[g] = packed_t[C3 + C1 * g : C3 + C1 * g + C1]

    def forward_three(g):
        out_t = yield from attend(q_three[g], k_three[g], vt_three[g], hot[0], 64, bias_three, g, probs_three, g)
        out_t_three[g] = out_t.astype(BF16)
        out_three[g] = jnp.transpose(out_t)[:ROWS].astype(BF16)

    together(forward_three(g) for g in range(4))
    out = jnp.concatenate([out_three[g] for g in range(4)], 1)
    cot_wide[...] = merged_two + rounded(dot(out, outward_three[...]))
    for frame in range(4):
        for row in range(7):
            group = (frame * 7 + row) * 8
            values = jnp.concatenate([cot_wide[group + 4 : group + 7, :], cot_wide[group : group + 4, :]], 0)
            section_stage[frame, row] = values.astype(BF16)
    for copy in section_copies:
        copy.start()

    cot_own.wait()
    for copy in (cot_ta, cot_both, cot_ha):
        copy.wait_recv()
    for frame in range(4):
        for row in range(7):
            source = cot_held[frame, row].astype(F32)
            group = (frame * 7 + row) * 8
            cot_wide[group : group + 4, :] = source[3:7]
            cot_wide[group + 4 : group + 7, :] = source[0:3]
            cot_wide[group + 7 : group + 8, :] = jnp.zeros((1, C3), F32)
    d_section = cot_wide[...]
    d_mixed = padded(d_section.astype(BF16))
    d_out = dot_t(d_mixed, outward_three[...]).astype(BF16)
    d_out_t = dot_t(outward_three[...], d_mixed)
    for g in range(4):
        d_out_three[g] = d_out[:, C1 * g : C1 * g + C1]
        d_out_t_three[g] = d_out_t[C1 * g : C1 * g + C1]

    def backward_three(g):
        d_packed_three[g] = yield from attend_pull(
            d_out_three[g],
            d_out_t_three[g],
            out_t_three[g].astype(F32),
            q_three[g],
            kt_three[g],
            v_three[g],
            probs_three,
            g,
        )

    together(backward_three(g) for g in range(4))
    d_packed = jnp.concatenate(
        [d_packed_three[g, :, C1 * part : C1 * part + C1] for part in range(3) for g in range(4)], 1
    )
    d_normed = rounded(dot_t(d_packed, projection_three[...]))
    d_merged_two = d_section + rounded(norm_pull(d_normed, hat_three, inverse_three, gain_three[...]))
    d_grouped_two = dot_t(d_merged_two.astype(BF16), merge_weight_two[...])
    d_merged_one = norm_pull(d_grouped_two, merged[...], inverse_two, merge_gain_two[...]).astype(BF16)
    for place in range(4):
        d_grouped = dot_t(d_merged_one[:, 256 * place : 256 * place + 256], merge_weight_one[...])
        grouped[place] = norm_pull(d_grouped, grouped[place], inverse_one[place][:, :1], merge_gain_one[...])

    def scatter_blocks(frame, _):
        for row in range(7):
            group = (frame * 7 + row) * 8
            for a in range(2):
                for b in range(2):
                    for p in range(2):
                        for q in range(2):
                            block = 2 * q + p
                            folded[frame, 2 + 4 * row + 2 * a + p, pl.ds(9 + 2 * b + q, 8, stride=4), :] = grouped[
                                2 * b + a, pl.ds(pl.multiple_of(group, 8), 8), 128 * block : 128 * block + 128
                            ]
        return 0

    lax.fori_loop(0, 4, scatter_blocks, 0)
    for frame in range(4):
        for row in range(2):
            back_out[frame, row] = folded[frame, 28 + row].astype(BF16)
    back.start()

    def backward_one(at):
        hat, inverse = normalised(windows[at])
        d_residual = rounded(mixed[at])
        d_mixed = padded(d_residual.astype(BF16))
        d_out = dot_t(d_mixed, outward_one[...]).astype(BF16)
        d_out_t = dot_t(outward_one[...], d_mixed)
        yield
        d_packed = yield from attend_pull(
            d_out, d_out_t, out_t_one[at].astype(F32), q_one[at], kt_one[at], v_one[at], probs_one, at
        )
        d_normed = rounded(dot_t(d_packed, projection_one[...]))
        mixed[at] = d_residual + norm_pull(d_normed, hat, inverse, gain_one[...])

    def backward_row(step, _):
        k = 3 - step

        @pl.when(k == 0)
        def _():
            back.wait_recv()
            for frame in range(4):
                for row in range(2):
                    folded[frame, row] = back_in[frame, row].astype(F32)

        for frame in range(4):
            for row in range(7):
                group = (frame * 7 + row) * 8
                folded[frame, 7 * k + row, 7:9, :] = folded[frame, 7 * k + row, 35:37, :]
                mixed[4 * k, group : group + 8, :] = folded[frame, 7 * k + row, 28:36, :]
                for m in range(1, 4):
                    mixed[4 * k + m, group : group + 8, :] = folded[frame, 7 * k + row, 7 * m : 7 * m + 8, :]

        together(backward_one(4 * k + m) for m in range(4))

        for frame in range(4):
            for row in range(7):
                group = (frame * 7 + row) * 8
                for m in range(3):
                    grid[frame, row, 3 + 7 * m : 10 + 7 * m, :] = mixed[4 * k + m, group : group + 7, :]
                grid[frame, row, 24:28, :] = mixed[4 * k + 3, group : group + 4, :]
                grid[frame, row, 0:3, :] = mixed[4 * k + 3, group + 4 : group + 7, :]
                grad_stage[frame, 7 * k + row] = grid[frame, row, 0:28, :].astype(BF16)

        for at in range(4):

            @pl.when(k == at)
            def _():
                for copy in grad_copies[at]:
                    copy.start()

        return 0

    lax.fori_loop(0, 4, backward_row, 0)

    early = (tokens_ta, tokens_ta_rest, tokens_ha, tokens_both, hot_ha, cot_ta, cot_ha, cot_both, seam, back)
    for copy in early:
        copy.wait_send()
    for copy in section_copies:
        copy.wait()
    for k in (3, 2, 1, 0):
        for copy in grad_copies[k]:
            copy.wait()


def main_call(mesh_shape, *operands):
    vmem = pl.BlockSpec(memory_space=pltpu.VMEM)
    hbm = pl.BlockSpec(memory_space=pl.ANY)
    in_specs = [hbm, vmem, vmem, vmem, vmem, vmem, vmem, vmem, vmem, vmem, hbm, vmem, hbm, vmem, hbm, hbm]
    return pl.pallas_call(
        functools.partial(main_kernel, *mesh_shape),
        out_shape=(
            jax.ShapeDtypeStruct((4, 7, 7, C3), BF16),
            jax.ShapeDtypeStruct((4, 28, 28, C1), BF16),
        ),
        in_specs=in_specs,
        out_specs=(hbm, hbm),
        scratch_shapes=[
            pltpu.VMEM((4, 28, 28, C1), BF16),
            pltpu.VMEM((4, 7, 7, C3), F32),
            pltpu.VMEM((4, 7, 7, C3), BF16),
            pltpu.VMEM((4, 7, 7, C3), BF16),
            pltpu.VMEM((2, ROWS, 128), BF16),
            pltpu.VMEM((4, 2, CELLS, C1), BF16),
            pltpu.VMEM((4, 2, CELLS, C1), BF16),
            pltpu.VMEM((4, 2, CELLS, C1), BF16),
            pltpu.VMEM((4, 2, CELLS, C1), BF16),
            pltpu.VMEM((4, 7, 7, C3), BF16),
            pltpu.VMEM((4, 28, 28, C1), BF16),
            pltpu.VMEM((4 * C1, 2 * C1), BF16),
            pltpu.VMEM((8 * C1, C3), BF16),
            pltpu.VMEM((C3, 3 * C3), BF16),
            pltpu.VMEM((C3, C3), BF16),
            pltpu.VMEM((2 * C1, C1), BF16),
            pltpu.VMEM((2 * C3, C3), BF16),
            pltpu.VMEM((1, 4 * ROWS, LANES), F32),
            pltpu.VMEM((4, 4 * ROWS, LANES), F32),
            pltpu.VMEM((4, 7, 40, C1), F32),
            pltpu.VMEM((4, 30, CELLS, C1), F32),
            pltpu.VMEM((WINDOWS, ROWS, C1), F32),
            pltpu.VMEM((WINDOWS, ROWS, C1), F32),
            pltpu.VMEM((WINDOWS, 4 * ROWS, LANES), BF16),
            pltpu.VMEM((WINDOWS, ROWS, C1), BF16),
            pltpu.VMEM((WINDOWS, C1, ROWS), BF16),
            pltpu.VMEM((WINDOWS, ROWS, C1), BF16),
            pltpu.VMEM((WINDOWS, C1, LANES), BF16),
            pltpu.VMEM((4, ROWS, 512), F32),
            pltpu.VMEM((4, ROWS, 128), F32),
            pltpu.VMEM((ROWS, 1024), F32),
            pltpu.VMEM((4, 4 * ROWS, LANES), BF16),
            pltpu.VMEM((4, ROWS, C1), BF16),
            pltpu.VMEM((4, ROWS, C1), BF16),
            pltpu.VMEM((4, ROWS, C1), BF16),
            pltpu.VMEM((4, C1, ROWS), BF16),
            pltpu.VMEM((4, C1, ROWS), BF16),
            pltpu.VMEM((4, C1, LANES), BF16),
            pltpu.VMEM((4, ROWS, C1), BF16),
            pltpu.VMEM((4, LANES, C1), BF16),
            pltpu.VMEM((4, C1, LANES), F32),
            pltpu.VMEM((4, ROWS, 3 * C1), BF16),
            pltpu.VMEM((ROWS, C3), F32),
            pltpu.VMEM((24, TABLE_LANES), F32),
            pltpu.VMEM((4 * ALL_HEADS * 8, DEPTH), F32),
            pltpu.SemaphoreType.DMA((20,)),
            pltpu.SemaphoreType.DMA((20,)),
            pltpu.SemaphoreType.DMA((12,)),
        ],
        compiler_params=pltpu.CompilerParams(
            vmem_limit_bytes=62 * 2**20, collective_id=0, has_side_effects=True
        ),
        cost_estimate=pl.CostEstimate(flops=3 * 10**10, bytes_accessed=2 * 10**7, transcendentals=4 * 10**6),
        name="sections",
    )(*operands)


def per_device(
    tokens,
    regions_one,
    regions_three,
    gain_one,
    projection_one,
    outward_one,
    table_one,
    merge_gain_one,
    merge_weight_one,
    merge_gain_two,
    merge_weight_two,
    gain_three,
    projection_three,
    outward_three,
    table_three,
    cotangent,
):
    return main_call(
        (lax.axis_size("ha"), lax.axis_size("ta")),
        tokens,
        cotangent.transpose(1, 2, 0, 3),
        regions_one.transpose(1, 0, 2),
        regions_three.transpose(1, 0, 2),
        table_one.T,
        table_three.T,
        gain_one.reshape(1, -1),
        projection_one,
        outward_one,
        merge_gain_one.reshape(1, -1),
        merge_weight_one,
        merge_gain_two.reshape(1, -1),
        merge_weight_two,
        gain_three.reshape(1, -1),
        projection_three,
        outward_three,
    )


def solution(mesh):
    wide = P(("col", "ta"), "ha", None, None)
    flat = P(("col", "ta"), "ha", None)
    in_specs = (wide, flat, flat) + (P(),) * 12 + (wide,)
    return jax.shard_map(per_device, mesh=mesh, in_specs=in_specs, out_specs=(wide, wide), check_vma=False)
```

```python
import functools
import math

import jax
import jax.numpy as jnp
from jax import lax
from jax.experimental import pallas as pl
from jax.experimental.pallas import tpu as pltpu
from jax.sharding import PartitionSpec as P

F32 = jnp.float32
BF16 = jnp.bfloat16

C1 = 128
C3 = 512
HEADS1 = 4
HEADS3 = 16
HEAD = 32
EPSILON = 1e-05

GROUPS = 28
ROWS = 224
LANES = 256
WINDOWS = 16
FIRST = 10
OWN = 28 - FIRST
CELLS = 48

LOG2E = math.log2(math.e)
LN2 = math.log(2.0)
SCALE = HEAD**-0.5
LEFT_OUT = 1e30

TABLE_LANES = 1408
OFFSETS = 1183
DEPTH = 768
ALL_HEADS = HEADS1 + HEADS3


def dot(a, b):
    return jnp.dot(a, b, preferred_element_type=F32)


def dot_t(a, b):
    return lax.dot_general(a, b, (((1,), (1,)), ((), ())), preferred_element_type=F32)


def normalised(x):
    centred = x - jnp.mean(x, -1, keepdims=True)
    inverse = lax.rsqrt(jnp.mean(centred * centred, -1, keepdims=True) + EPSILON)
    return centred * inverse, inverse


def norm_pull(grad, hat, inverse, gain):
    scaled = grad * gain
    mean = jnp.mean(scaled, -1, keepdims=True)
    along = jnp.mean(scaled * hat, -1, keepdims=True)
    return inverse * (scaled - mean - hat * along)


def rounded(x):
    return x.astype(BF16).astype(F32)


def head_mask(head):
    lane = lax.broadcasted_iota(jnp.int32, (1, C1), 1)
    return jnp.where((lane >= HEAD * head) & (lane < HEAD * (head + 1)), 1.0, 0.0).astype(BF16)


def padded(x):
    return jnp.concatenate([x, jnp.zeros((LANES - ROWS, x.shape[1]), x.dtype)], 0)


def attend(q, k, values_t, hot, hot_at, bias_ref, bias_at, probs_ref, at):
    lane = lax.broadcasted_iota(jnp.int32, (1, 128), 1)
    chosen = jnp.where((lane >= hot_at) & (lane < hot_at + 4), LEFT_OUT, 0.0).astype(BF16)
    q_wide = jnp.concatenate([padded(q), padded((hot - 1.0) * chosen)], 1)
    k_wide = jnp.concatenate([jnp.concatenate([k * head_mask(head), hot], 1) for head in range(4)], 0)
    scores = dot_t(k_wide, q_wide)
    yield
    out = []
    for head in range(4):
        rows = slice(ROWS * head, ROWS * head + ROWS)
        for half in range(2):
            lanes = slice(128 * half, 128 * half + 128)
            part = scores[rows, lanes] + bias_ref[bias_at, rows, lanes]
            raised = jnp.exp2(part - jnp.max(part, 0, keepdims=True))
            share = 1.0 / jnp.sum(raised, 0, keepdims=True)
            probs_ref[at, rows, lanes] = (raised * share).astype(BF16)
        yield
        out.append(dot(values_t[HEAD * head : HEAD * head + HEAD], probs_ref[at, rows, :]))
    return jnp.concatenate(out, 0)


def attend_pull(d_out, d_out_t, out_t, q, keys_t, values, probs_ref, at):
    product = d_out_t * out_t
    values = jnp.concatenate([values * head_mask(head) for head in range(4)], 0)
    d_probs = dot_t(values, d_out)
    yield
    d_queries = []
    d_scores = []
    for head in range(4):
        rows = slice(ROWS * head, ROWS * head + ROWS)
        own = slice(HEAD * head, HEAD * head + HEAD)
        delta = jnp.sum(product[own], 0, keepdims=True)
        d_scores.append((probs_ref[at, rows, :].astype(F32) * (d_probs[rows] - delta)).astype(BF16))
        yield
        d_queries.append(dot(keys_t[own], d_scores[head]))
    all_values = dot(probs_ref[at], d_out)
    all_keys = dot(jnp.concatenate(d_scores, 0), padded(q))
    yield
    d_values = pick_heads(all_values)
    d_keys = pick_heads(all_keys) * LN2
    d_q = jnp.transpose(jnp.concatenate(d_queries, 0) * SCALE)[:ROWS]
    return jnp.concatenate([d_q.astype(BF16), d_keys.astype(BF16), d_values.astype(BF16)], 1)


def together(parts):
    parts = list(parts)
    while parts:
        parts = [part for part in parts if next(part, parts) is None]


def pick_heads(stacked):
    lane = lax.broadcasted_iota(jnp.int32, (1, C1), 1)
    result = stacked[3 * ROWS :]
    for head in (2, 1, 0):
        result = jnp.where(lane < HEAD * (head + 1), stacked[ROWS * head : ROWS * head + ROWS], result)
    return result


def expand_tables(table_one, table_three, one_ref, three_ref, table_ref, wide_ref):
    table_ref[...] = jnp.zeros((24, TABLE_LANES), F32)
    table_ref[0:HEADS1, 8 : 8 + OFFSETS] = table_one[...]
    table_ref[8:24, 8 : 8 + OFFSETS] = table_three[...]
    for head in range(ALL_HEADS):
        held_at = head if head < HEADS1 else head + 8 - HEADS1
        row = jnp.broadcast_to(table_ref[held_at : held_at + 1, :] * LOG2E, (8, TABLE_LANES))
        for frame in range(4):
            start = 14 + 169 * (3 - frame)
            moved = pltpu.roll(row, TABLE_LANES - start, 1, stride=1, stride_axis=0)
            first = (frame * ALL_HEADS + head) * 8
            wide_ref[first : first + 8, :] = moved[:, :DEPTH]
    wide = wide_ref[...]
    high = wide.astype(BF16)
    low = (wide - high.astype(F32)).astype(BF16)
    lane = lax.broadcasted_iota(jnp.int32, (DEPTH, LANES), 1)
    depth = lax.broadcasted_iota(jnp.int32, (DEPTH, LANES), 0)
    group = lane >> 3
    column = lane & 7
    frame = (group * 9363) >> 16
    line = group - 7 * frame
    offset = 169 * frame + 13 * line + column
    valid = (column < 7) & (lane < ROWS)
    for key_line in range(7):
        chosen = valid & (depth == offset + 13 * (6 - key_line))
        chosen = jnp.where(chosen, 1.0, 0.0).astype(BF16)
        picked = dot(high, chosen) + dot(low, chosen)
        for key_frame in range(4):
            to = key_frame * 56 + key_line * 8
            for head in range(ALL_HEADS):
                first = (key_frame * ALL_HEADS + head) * 8
                block = picked[first : first + 8]
                if head < HEADS1:
                    one_ref[0, head * ROWS + to : head * ROWS + to + 8, :] = block
                else:
                    group_at, place = divmod(head - HEADS1, 4)
                    three_ref[group_at, place * ROWS + to : place * ROWS + to + 8, :] = block


def region_classes(one_ref, three_ref, hot_ref):
    def spread(ref, first, width, lane_of):
        place = lax.broadcasted_iota(jnp.int32, (8, width), 0)
        column = lax.broadcasted_iota(jnp.int32, (8, width), 1)
        own = jnp.where(column - 7 * ((column * 37) >> 8) == place, 1.0, 0.0)
        ids = [ref[first + row, frame : frame + 1, :].astype(F32) * own for frame in range(4) for row in range(7)]
        column = lax.broadcasted_iota(jnp.int32, (width, 128), 0)
        lane = lax.broadcasted_iota(jnp.int32, (width, 128), 1)
        target = jnp.where((lane >> 2) == lane_of + ((column * 37) >> 8), 1.0, 0.0).astype(BF16)
        return dot(jnp.concatenate(ids, 0).astype(BF16), target)

    ids = spread(three_ref, 0, 7, WINDOWS)
    for k in range(4):
        ids += spread(one_ref, 7 * k, 28, 4 * k)
    lane = lax.broadcasted_iota(jnp.int32, (ROWS, 128), 1) & 3
    place = lax.broadcasted_iota(jnp.int32, (ROWS, 128), 0) & 7
    ids = jnp.where(place == 7, 3.0, ids)
    hot_ref[0] = jnp.where(ids == lane.astype(F32), 1.0, 0.0).astype(BF16)


def main_kernel(
    ha_count,
    ta_count,
    tokens,
    cotangent,
    regions_one,
    regions_three,
    table_one,
    table_three,
    gain_one,
    projection_one,
    outward_one,
    merge_gain_one,
    merge_weight_one_hbm,
    merge_gain_two,
    merge_weight_two_hbm,
    gain_three,
    projection_three_hbm,
    outward_three_hbm,
    section_out,
    grad_out,
    held,
    cot_rows,
    cot_stage,
    cot_held,
    hot,
    seam_out,
    seam_in,
    back_out,
    back_in,
    section_stage,
    grad_stage,
    merge_weight_one,
    merge_weight_two,
    projection_three,
    outward_three,
    kv_one_t,
    kv_three_t,
    bias_one,
    bias_three,
    grid,
    folded,
    windows,
    mixed,
    probs_one,
    q_one,
    kt_one,
    v_one,
    out_t_one,
    grouped,
    inverse_one,
    merged,
    probs_three,
    q_three,
    k_three,
    v_three,
    kt_three,
    vt_three,
    out_t_three,
    out_three,
    d_out_three,
    d_out_t_three,
    d_packed_three,
    cot_wide,
    tables,
    wide,
    send_sems,
    receive_sems,
    own_sems,
):
    ha, ta = lax.axis_index("ha"), lax.axis_index("ta")
    ha_next, ha_last = lax.rem(ha + 1, ha_count), lax.rem(ha + ha_count - 1, ha_count)
    ta_next, ta_last = lax.rem(ta + 1, ta_count), lax.rem(ta + ta_count - 1, ta_count)

    barrier = pltpu.get_barrier_semaphore()
    ahead = ({"ta": ta_next}, {"ha": ha_next}, {"ha": ha_next, "ta": ta_next})
    behind = ({"ta": ta_last}, {"ha": ha_last}, {"ha": ha_last, "ta": ta_last})

    sent = []

    def remote(source, target, device):
        at = len(sent)
        sent.append(
            pltpu.make_async_remote_copy(
                src_ref=source,
                dst_ref=target,
                send_sem=send_sems.at[at],
                recv_sem=receive_sems.at[at],
                device_id=device,
                device_id_type=pl.DeviceIdType.MESH,
            )
        )
        return sent[-1]

    moved = []

    def local(source, target):
        moved.append(pltpu.make_async_copy(source, target, own_sems.at[len(moved)]))
        return moved[-1]

    tokens_own = local(tokens.at[2:4, FIRST:28], held.at[0:2, 0:OWN])
    cot_own = local(cot_stage.at[2:4, 3:7], cot_held.at[0:2, 0:4])
    weights = [
        local(projection_three_hbm, projection_three),
        local(merge_weight_one_hbm, merge_weight_one),
        local(merge_weight_two_hbm, merge_weight_two),
        local(outward_three_hbm, outward_three),
    ]
    tokens_ta = remote(tokens.at[0:2, FIRST : FIRST + 7], held.at[2:4, 0:7], behind[0])
    tokens_ta_rest = remote(tokens.at[0:2, FIRST + 7 : 28], held.at[2:4, 7:OWN], behind[0])
    tokens_ha = remote(tokens.at[2:4, 0:FIRST], held.at[0:2, OWN:28], behind[1])
    tokens_both = remote(tokens.at[0:2, 0:FIRST], held.at[2:4, OWN:28], behind[2])
    hot_ha = remote(hot.at[0], hot.at[1], behind[1])
    cot_ta = remote(cot_stage.at[0:2, 3:7], cot_held.at[2:4, 0:4], behind[0])
    cot_ha = remote(cot_stage.at[2:4, 0:3], cot_held.at[0:2, 4:7], behind[1])
    cot_both = remote(cot_stage.at[0:2, 0:3], cot_held.at[2:4, 4:7], behind[2])
    seam = remote(seam_out, seam_in, behind[1])
    back = remote(back_out, back_in, ahead[1])
    section_copies = [
        remote(section_stage.at[2:4, 0:4], section_out.at[0:2, 3:7], ahead[0]),
        remote(section_stage.at[0:2, 4:7], section_out.at[2:4, 0:3], ahead[1]),
        remote(section_stage.at[2:4, 4:7], section_out.at[0:2, 0:3], ahead[2]),
        local(section_stage.at[0:2, 0:4], section_out.at[2:4, 3:7]),
    ]
    grad_copies = {3: [], 2: [], 1: [], 0: []}
    for k, low, high in ((3, 21, 28), (2, 18, 21)):
        to = slice(low - OWN, high - OWN)
        grad_copies[k].append(remote(grad_stage.at[2:4, low:high], grad_out.at[0:2, to], ahead[2]))
        grad_copies[k].append(remote(grad_stage.at[0:2, low:high], grad_out.at[2:4, to], ahead[1]))
    for k, low, high in ((2, 14, 18), (1, 7, 14), (0, 0, 7)):
        to = slice(low + FIRST, high + FIRST)
        grad_copies[k].append(remote(grad_stage.at[2:4, low:high], grad_out.at[0:2, to], ahead[0]))
        grad_copies[k].append(local(grad_stage.at[0:2, low:high], grad_out.at[2:4, to]))

    tokens_own.start()
    for device in ahead + behind:
        pl.semaphore_signal(barrier, inc=1, device_id=device, device_id_type=pl.DeviceIdType.MESH)
    pl.semaphore_wait(barrier, 6)
    for copy in (tokens_ta, tokens_ha):
        copy.start()
    for copy in weights:
        copy.start()

    region_classes(regions_one, regions_three, hot)
    for row in range(7):
        source = cotangent[row].astype(F32)
        for column in range(7):
            for frame in range(4):
                cot_rows[frame, row, column : column + 1, :] = source[column, frame : frame + 1, :]
        for frame in range(4):
            cot_stage[frame, row] = cot_rows[frame, row].astype(BF16)
    tokens_ta_rest.start()
    cot_own.start()
    expand_tables(table_one, table_three, bias_one, bias_three, tables, wide)
    for copy in (tokens_both, hot_ha, cot_ta, cot_ha, cot_both):
        copy.start()
    for part in range(2):
        weight = projection_one[:, C1 * (part + 1) : C1 * (part + 2)].astype(F32)
        kv_one_t[C1 * part : C1 * part + C1, :] = jnp.transpose(weight).astype(BF16)
    weights[0].wait()
    for part in range(8):
        weight = projection_three[:, C3 + C1 * part : C3 + C1 * part + C1].astype(F32)
        kv_three_t[C1 * part : C1 * part + C1, :] = jnp.transpose(weight).astype(BF16)
    tokens_own.wait()

    def forward_one(k, m):
        at = 4 * k + m
        x = windows[at]
        hat, _unused = normalised(x)
        normed = (hat * gain_one[...]).astype(BF16)
        yield
        packed = dot(normed, projection_one[...])
        packed_t = dot_t(kv_one_t[...], normed).astype(BF16)
        yield
        q = (packed[:, :C1] * (SCALE * LOG2E)).astype(BF16)
        v_one[at] = packed[:, 2 * C1 :].astype(BF16)
        q_one[at] = q
        kt_one[at] = packed_t[:C1]
        hot_at = 4 * (4 * lax.rem(k + 1, 4) + m)
        out_t = yield from attend(
            q,
            packed[:, C1 : 2 * C1].astype(BF16),
            packed_t[C1:],
            hot[k // 3],
            hot_at,
            bias_one,
            0,
            probs_one,
            at,
        )
        yield
        out_t_one[at] = out_t.astype(BF16)
        out = jnp.transpose(out_t)[:ROWS].astype(BF16)
        mixed[at] = rounded(x + rounded(dot(out, outward_one[...])))

    def forward_row(k, _):
        @pl.when(k == 0)
        def _():
            tokens_ta.wait_recv()

        @pl.when(k == 1)
        def _():
            tokens_ta_rest.wait_recv()

        @pl.when(k == 2)
        def _():
            tokens_both.wait_recv()
            tokens_ha.wait_recv()

        @pl.when(k == 3)
        def _():
            hot_ha.wait_recv()

        for frame in range(4):
            for row in range(7):
                values = held[frame, 7 * k + row].astype(F32)
                grid[frame, row, 0:28, :] = values
                grid[frame, row, 28:36, :] = values[0:8]
                group = (frame * 7 + row) * 8
                for m in range(4):
                    windows[4 * k + m, group : group + 8, :] = grid[frame, row, 3 + 7 * m : 11 + 7 * m, :]

        together(forward_one(k, m) for m in range(4))

        for frame in range(4):
            for row in range(7):
                group = (frame * 7 + row) * 8
                folded[frame, 7 * k + row, 28:35, :] = mixed[4 * k, group : group + 7, :]
                second = mixed[4 * k + 1, group : group + 7, :]
                folded[frame, 7 * k + row, 7:14, :] = second
                folded[frame, 7 * k + row, 35:42, :] = second
                folded[frame, 7 * k + row, 14:21, :] = mixed[4 * k + 2, group : group + 7, :]
                folded[frame, 7 * k + row, 21:28, :] = mixed[4 * k + 3, group : group + 7, :]

        @pl.when(k == 0)
        def _():
            for frame in range(4):
                for row in range(2):
                    seam_out[frame, row] = folded[frame, row].astype(BF16)
            seam.start()

        return 0

    lax.fori_loop(0, 4, forward_row, 0)
    seam.wait_recv()
    for frame in range(4):
        for row in range(2):
            folded[frame, 28 + row] = seam_in[frame, row].astype(F32)
    for copy in weights[1:]:
        copy.wait()

    def gather_blocks(frame, _):
        for row in range(7):
            group = (frame * 7 + row) * 8
            for a in range(2):
                for b in range(2):
                    for p in range(2):
                        for q in range(2):
                            block = 2 * q + p
                            grouped[2 * b + a, pl.ds(pl.multiple_of(group, 8), 8), 128 * block : 128 * block + 128] = folded[
                                frame, 2 + 4 * row + 2 * a + p, pl.ds(9 + 2 * b + q, 8, stride=4), :
                            ]
        return 0

    lax.fori_loop(0, 4, gather_blocks, 0)

    for place in range(4):
        hat, inverse = normalised(grouped[place])
        grouped[place] = hat
        inverse_one[place] = jnp.broadcast_to(inverse, (ROWS, 128))
        merged[:, 256 * place : 256 * place + 256] = rounded(
            dot((hat * merge_gain_one[...]).astype(BF16), merge_weight_one[...])
        )
    hat_two, inverse_two = normalised(merged[...])
    merged[...] = hat_two
    merged_two = rounded(dot((hat_two * merge_gain_two[...]).astype(BF16), merge_weight_two[...]))
    hat_three, inverse_three = normalised(merged_two)
    normed_three = (hat_three * gain_three[...]).astype(BF16)

    packed = dot(normed_three, projection_three[...])
    packed_t = dot_t(kv_three_t[...], normed_three).astype(BF16)
    for g in range(4):
        q_three[g] = (packed[:, C1 * g : C1 * g + C1] * (SCALE * LOG2E)).astype(BF16)
        k_three[g] = packed[:, C3 + C1 * g : C3 + C1 * g + C1].astype(BF16)
        v_three[g] = packed[:, 2 * C3 + C1 * g : 2 * C3 + C1 * g + C1].astype(BF16)
        kt_three[g] = packed_t[C1 * g : C1 * g + C1]
        vt_three[g] = packed_t[C3 + C1 * g : C3 + C1 * g + C1]

    def forward_three(g):
        out_t = yield from attend(q_three[g], k_three[g], vt_three[g], hot[0], 64, bias_three, g, probs_three, g)
        out_t_three[g] = out_t.astype(BF16)
        out_three[g] = jnp.transpose(out_t)[:ROWS].astype(BF16)

    together(forward_three(g) for g in range(4))
    out = jnp.concatenate([out_three[g] for g in range(4)], 1)
    cot_wide[...] = merged_two + rounded(dot(out, outward_three[...]))
    for frame in range(4):
        for row in range(7):
            group = (frame * 7 + row) * 8
            values = jnp.concatenate([cot_wide[group + 4 : group + 7, :], cot_wide[group : group + 4, :]], 0)
            section_stage[frame, row] = values.astype(BF16)
    for copy in section_copies:
        copy.start()

    cot_own.wait()
    for copy in (cot_ta, cot_both, cot_ha):
        copy.wait_recv()
    for frame in range(4):
        for row in range(7):
            source = cot_held[frame, row].astype(F32)
            group = (frame * 7 + row) * 8
            cot_wide[group : group + 4, :] = source[3:7]
            cot_wide[group + 4 : group + 7, :] = source[0:3]
            cot_wide[group + 7 : group + 8, :] = jnp.zeros((1, C3), F32)
    d_section = cot_wide[...]
    d_mixed = padded(d_section.astype(BF16))
    d_out = dot_t(d_mixed, outward_three[...]).astype(BF16)
    d_out_t = dot_t(outward_three[...], d_mixed)
    for g in range(4):
        d_out_three[g] = d_out[:, C1 * g : C1 * g + C1]
        d_out_t_three[g] = d_out_t[C1 * g : C1 * g + C1]

    def backward_three(g):
        d_packed_three[g] = yield from attend_pull(
            d_out_three[g],
            d_out_t_three[g],
            out_t_three[g].astype(F32),
            q_three[g],
            kt_three[g],
            v_three[g],
            probs_three,
            g,
        )

    together(backward_three(g) for g in range(4))
    d_packed = jnp.concatenate(
        [d_packed_three[g, :, C1 * part : C1 * part + C1] for part in range(3) for g in range(4)], 1
    )
    d_normed = rounded(dot_t(d_packed, projection_three[...]))
    d_merged_two = d_section + rounded(norm_pull(d_normed, hat_three, inverse_three, gain_three[...]))
    d_grouped_two = dot_t(d_merged_two.astype(BF16), merge_weight_two[...])
    d_merged_one = norm_pull(d_grouped_two, merged[...], inverse_two, merge_gain_two[...]).astype(BF16)
    for place in range(4):
        d_grouped = dot_t(d_merged_one[:, 256 * place : 256 * place + 256], merge_weight_one[...])
        grouped[place] = norm_pull(d_grouped, grouped[place], inverse_one[place][:, :1], merge_gain_one[...])

    def scatter_blocks(frame, _):
        for row in range(7):
            group = (frame * 7 + row) * 8
            for a in range(2):
                for b in range(2):
                    for p in range(2):
                        for q in range(2):
                            block = 2 * q + p
                            folded[frame, 2 + 4 * row + 2 * a + p, pl.ds(9 + 2 * b + q, 8, stride=4), :] = grouped[
                                2 * b + a, pl.ds(pl.multiple_of(group, 8), 8), 128 * block : 128 * block + 128
                            ]
        return 0

    lax.fori_loop(0, 4, scatter_blocks, 0)
    for frame in range(4):
        for row in range(2):
            back_out[frame, row] = folded[frame, 28 + row].astype(BF16)
    back.start()

    def backward_one(at):
        hat, inverse = normalised(windows[at])
        d_residual = rounded(mixed[at])
        d_mixed = padded(d_residual.astype(BF16))
        d_out = dot_t(d_mixed, outward_one[...]).astype(BF16)
        d_out_t = dot_t(outward_one[...], d_mixed)
        yield
        d_packed = yield from attend_pull(
            d_out, d_out_t, out_t_one[at].astype(F32), q_one[at], kt_one[at], v_one[at], probs_one, at
        )
        d_normed = rounded(dot_t(d_packed, projection_one[...]))
        mixed[at] = d_residual + norm_pull(d_normed, hat, inverse, gain_one[...])

    def backward_row(step, _):
        k = 3 - step

        @pl.when(k == 0)
        def _():
            back.wait_recv()
            for frame in range(4):
                for row in range(2):
                    folded[frame, row] = back_in[frame, row].astype(F32)

        for frame in range(4):
            for row in range(7):
                group = (frame * 7 + row) * 8
                folded[frame, 7 * k + row, 7:9, :] = folded[frame, 7 * k + row, 35:37, :]
                mixed[4 * k, group : group + 8, :] = folded[frame, 7 * k + row, 28:36, :]
                for m in range(1, 4):
                    mixed[4 * k + m, group : group + 8, :] = folded[frame, 7 * k + row, 7 * m : 7 * m + 8, :]

        together(backward_one(4 * k + m) for m in range(4))

        for frame in range(4):
            for row in range(7):
                group = (frame * 7 + row) * 8
                for m in range(3):
                    grid[frame, row, 3 + 7 * m : 10 + 7 * m, :] = mixed[4 * k + m, group : group + 7, :]
                grid[frame, row, 24:28, :] = mixed[4 * k + 3, group : group + 4, :]
                grid[frame, row, 0:3, :] = mixed[4 * k + 3, group + 4 : group + 7, :]
                grad_stage[frame, 7 * k + row] = grid[frame, row, 0:28, :].astype(BF16)

        for at in range(4):

            @pl.when(k == at)
            def _():
                for copy in grad_copies[at]:
                    copy.start()

        return 0

    lax.fori_loop(0, 4, backward_row, 0)

    early = (tokens_ta, tokens_ta_rest, tokens_ha, tokens_both, hot_ha, cot_ta, cot_ha, cot_both, seam, back)
    for copy in early:
        copy.wait_send()
    for copy in section_copies:
        copy.wait()
    for k in (3, 2, 1, 0):
        for copy in grad_copies[k]:
            copy.wait()


def main_call(mesh_shape, *operands):
    vmem = pl.BlockSpec(memory_space=pltpu.VMEM)
    hbm = pl.BlockSpec(memory_space=pl.ANY)
    in_specs = [hbm, vmem, vmem, vmem, vmem, vmem, vmem, vmem, vmem, vmem, hbm, vmem, hbm, vmem, hbm, hbm]
    return pl.pallas_call(
        functools.partial(main_kernel, *mesh_shape),
        out_shape=(
            jax.ShapeDtypeStruct((4, 7, 7, C3), BF16),
            jax.ShapeDtypeStruct((4, 28, 28, C1), BF16),
        ),
        in_specs=in_specs,
        out_specs=(hbm, hbm),
        scratch_shapes=[
            pltpu.VMEM((4, 28, 28, C1), BF16),
            pltpu.VMEM((4, 7, 7, C3), F32),
            pltpu.VMEM((4, 7, 7, C3), BF16),
            pltpu.VMEM((4, 7, 7, C3), BF16),
            pltpu.VMEM((2, ROWS, 128), BF16),
            pltpu.VMEM((4, 2, CELLS, C1), BF16),
            pltpu.VMEM((4, 2, CELLS, C1), BF16),
            pltpu.VMEM((4, 2, CELLS, C1), BF16),
            pltpu.VMEM((4, 2, CELLS, C1), BF16),
            pltpu.VMEM((4, 7, 7, C3), BF16),
            pltpu.VMEM((4, 28, 28, C1), BF16),
            pltpu.VMEM((4 * C1, 2 * C1), BF16),
            pltpu.VMEM((8 * C1, C3), BF16),
            pltpu.VMEM((C3, 3 * C3), BF16),
            pltpu.VMEM((C3, C3), BF16),
            pltpu.VMEM((2 * C1, C1), BF16),
            pltpu.VMEM((2 * C3, C3), BF16),
            pltpu.VMEM((1, 4 * ROWS, LANES), F32),
            pltpu.VMEM((4, 4 * ROWS, LANES), F32),
            pltpu.VMEM((4, 7, 40, C1), F32),
            pltpu.VMEM((4, 30, CELLS, C1), F32),
            pltpu.VMEM((WINDOWS, ROWS, C1), F32),
            pltpu.VMEM((WINDOWS, ROWS, C1), F32),
            pltpu.VMEM((WINDOWS, 4 * ROWS, LANES), BF16),
            pltpu.VMEM((WINDOWS, ROWS, C1), BF16),
            pltpu.VMEM((WINDOWS, C1, ROWS), BF16),
            pltpu.VMEM((WINDOWS, ROWS, C1), BF16),
            pltpu.VMEM((WINDOWS, C1, LANES), BF16),
            pltpu.VMEM((4, ROWS, 512), F32),
            pltpu.VMEM((4, ROWS, 128), F32),
            pltpu.VMEM((ROWS, 1024), F32),
            pltpu.VMEM((4, 4 * ROWS, LANES), BF16),
            pltpu.VMEM((4, ROWS, C1), BF16),
            pltpu.VMEM((4, ROWS, C1), BF16),
            pltpu.VMEM((4, ROWS, C1), BF16),
            pltpu.VMEM((4, C1, ROWS), BF16),
            pltpu.VMEM((4, C1, ROWS), BF16),
            pltpu.VMEM((4, C1, LANES), BF16),
            pltpu.VMEM((4, ROWS, C1), BF16),
            pltpu.VMEM((4, LANES, C1), BF16),
            pltpu.VMEM((4, C1, LANES), F32),
            pltpu.VMEM((4, ROWS, 3 * C1), BF16),
            pltpu.VMEM((ROWS, C3), F32),
            pltpu.VMEM((24, TABLE_LANES), F32),
            pltpu.VMEM((4 * ALL_HEADS * 8, DEPTH), F32),
            pltpu.SemaphoreType.DMA((20,)),
            pltpu.SemaphoreType.DMA((20,)),
            pltpu.SemaphoreType.DMA((12,)),
        ],
        compiler_params=pltpu.CompilerParams(
            vmem_limit_bytes=62 * 2**20, collective_id=0, has_side_effects=True
        ),
        cost_estimate=pl.CostEstimate(flops=3 * 10**10, bytes_accessed=2 * 10**7, transcendentals=4 * 10**6),
        name="sections",
    )(*operands)


def per_device(
    tokens,
    regions_one,
    regions_three,
    gain_one,
    projection_one,
    outward_one,
    table_one,
    merge_gain_one,
    merge_weight_one,
    merge_gain_two,
    merge_weight_two,
    gain_three,
    projection_three,
    outward_three,
    table_three,
    cotangent,
):
    return main_call(
        (lax.axis_size("ha"), lax.axis_size("ta")),
        tokens,
        cotangent.transpose(1, 2, 0, 3),
        regions_one.transpose(1, 0, 2),
        regions_three.transpose(1, 0, 2),
        table_one.T,
        table_three.T,
        gain_one.reshape(1, -1),
        projection_one,
        outward_one,
        merge_gain_one.reshape(1, -1),
        merge_weight_one,
        merge_gain_two.reshape(1, -1),
        merge_weight_two,
        gain_three.reshape(1, -1),
        projection_three,
        outward_three,
    )


def solution(mesh):
    wide = P(("col", "ta"), "ha", None, None)
    flat = P(("col", "ta"), "ha", None)
    in_specs = (wide, flat, flat) + (P(),) * 12 + (wide,)
    return jax.shard_map(per_device, mesh=mesh, in_specs=in_specs, out_specs=(wide, wide), check_vma=False)
```
